128 devices in a mesh: row: 16 (over x_lo, z, core), col: 8 (over y, x_hi).
Axes of the slice: x: 4 (x_hi: 2, x_lo: 2; x = x_hi * 2 + x_lo), y: 4, z: 4, core: 2. Of those that a mesh axis runs over, the one named last changes fastest.
Arguments:
- features: bfloat16 [16384, 768], P(('col', 'row')), may hold values from -6 to 6
- w_neigh: bfloat16 [768, 1024], replicated, may hold values from -0.875 to 0.875
- w_self: bfloat16 [768, 1024], replicated, may hold values from -0.21875 to 0.21875
- bias: float32 [1024], replicated, may hold values from -3 to 3
- cotangent: bfloat16 [16384, 1024], P(('row', 'col')), may hold values from -6 to 6
- block_rows: int32 [16, 8, 96], P('row', 'col'), may hold values from 0 to 7
- block_cols: int32 [16, 8, 96], P('row', 'col'), may hold values from 0 to 15
- block_vals: bfloat16 [16, 8, 96, 128, 128], P('row', 'col'), may hold values from 0 to 1, as said below
- block_count: int32 [16, 8], P('row', 'col'), may hold values from 24 to 96, as said below
Outputs:
- output: bfloat16 [16384, 1024], P(('row', 'col'))
- grad_input: bfloat16 [16384, 768], P(('col', 'row'))
- grad_self: float32 [768, 1024], replicated
- grad_neigh: float32 [768, 1024], replicated
- grad_bias: float32 [1024], replicated
The draws below stay inside these ranges and needn't reach their ends.
Inputs may be any that keep to these rules, and one draw needn't show every extreme that they name: `block_vals`: block values are non-negative edge weights. `block_count`: some tile in every draw has all 96 slots live.
All inputs are finite; a program needn't handle non-finite values.
Results may differ from the reference program's by a relative error of at most 0.0053.
Values may be sent and summed in bfloat16 or wider, within the bound.
A program may use at most 128 MiB of HBM per device.

```python
import math
import jax
import jax.numpy as jnp
from jax import lax

D = 768
HID = 1024
NODE_DEV = 128
BLK = 128
NODES = 16384
TB_R = 8
TB_C = 16
NBLK = 96
N_ROW = 16
N_COL = 8


def draw_block_vals(key, part):
    key = jax.random.fold_in(key, 7)
    first_key, second_key = jax.random.split(key)
    shape = (N_ROW, N_COL, NBLK, BLK, BLK)
    keep_mask = jax.random.randint(first_key, shape, 0, 8) == 0
    magnitude = jnp.exp(jax.random.uniform(second_key, shape, jnp.float32, math.log(0.25), 0.0))
    return jnp.where(keep_mask, magnitude, 0.0).astype(jnp.bfloat16)


def draw_block_count(key, part):
    key = jax.random.fold_in(key, 11)
    first_key, second_key = jax.random.split(key)
    counts = jax.random.randint(first_key, (N_ROW * N_COL,), NBLK // 4, NBLK + 1)
    busiest = jax.random.randint(second_key, (), 0, N_ROW * N_COL)
    flattened = jnp.where(jnp.arange(N_ROW * N_COL) == busiest, NBLK, counts)
    return flattened.reshape(N_ROW, N_COL).astype(jnp.int32)


def with_ends(entries, key, low, top_value):
    dims = entries.shape
    place = [jax.random.randint(jax.random.fold_in(key, axis), (), 0, dims[axis]) for axis in range(len(dims))]
    entries = entries.at[tuple(place)].set(low)
    longest = dims.index(max(dims))
    place[longest] = (place[longest] + 1) % dims[longest]
    return entries.at[tuple(place)].set(top_value)


def levels(own_key, shape, cuts, smallest, high):
    level = 1.0
    for dim, blocks in cuts:
        steps = jax.random.uniform(jax.random.fold_in(jax.random.fold_in(own_key, 6), dim), (blocks,), jnp.float32, smallest / len(cuts), high / len(cuts))
        level = level * jnp.repeat(jnp.exp(steps), shape[dim] // blocks).reshape((-1,) + (1,) * (len(shape) - 1 - dim))
    return level


def noise(stream_key, dims, scale, reach, cuts=(), held_as=jnp.bfloat16):
    loudness = levels(stream_key, dims, cuts, -0.22, 0.18) if cuts else 1.0
    array = jax.random.normal(stream_key, dims, jnp.float32) * scale * loudness
    return jnp.minimum(jnp.maximum(array, -reach), reach).astype(held_as)


def setup_inputs(seed: int = 0) -> dict:
    splits = jax.random.split(jax.random.key(seed), 10)
    features = noise(splits[0], (NODES, D), 1.0, 6.0, ((0, 128),))
    w_neigh = noise(splits[1], (D, HID), (D // 16) ** -0.5, 0.875)
    w_self = noise(splits[2], (D, HID), D ** -0.5, 0.21875)
    bias = noise(splits[3], (HID,), 0.5, 3.0, (), jnp.float32)
    cotangent = noise(splits[4], (NODES, HID), 1.0, 6.0, ((0, 128),))
    block_rows = with_ends(jax.random.randint(splits[5], (N_ROW, N_COL, NBLK), 0, TB_R), jax.random.fold_in(splits[5], 1), 0, TB_R - 1).astype(jnp.int32)
    block_cols = with_ends(jax.random.randint(splits[6], (N_ROW, N_COL, NBLK), 0, TB_C), jax.random.fold_in(splits[6], 1), 0, TB_C - 1).astype(jnp.int32)
    block_vals = draw_block_vals(jax.random.fold_in(splits[9], 71), 0)
    block_count = draw_block_count(jax.random.fold_in(splits[9], 71), 0)
    return dict(features=features, w_neigh=w_neigh, w_self=w_self, bias=bias, cotangent=cotangent, block_rows=block_rows, block_cols=block_cols, block_vals=block_vals, block_count=block_count)


def block_term(block_vals, take_ids, put_ids, live_count, source, seg_count, flipped, start_slot, group_size):
    chosen = lax.dynamic_slice_in_dim(block_vals, start_slot, group_size, 0)
    taken = lax.dynamic_slice_in_dim(take_ids, start_slot, group_size, 0)
    placed = lax.dynamic_slice_in_dim(put_ids, start_slot, group_size, 0)
    slot_ids = start_slot + jnp.arange(group_size, dtype=jnp.int32)
    live_mask = (slot_ids < live_count).astype(jnp.float32)
    weights = chosen.astype(jnp.float32) * live_mask[:, None, None]
    gathered = source[taken].astype(jnp.float32)
    pattern = 'gji,gjw->giw' if flipped else 'gij,gjw->giw'
    products = jnp.einsum(pattern, weights, gathered)
    return jax.ops.segment_sum(products, placed, num_segments=seg_count)

def sparse_product(block_vals, take_ids, put_ids, live_count, source, seg_count, flipped):
    slot_total = block_vals.shape[0]
    group_size = min(8, slot_total)
    width = source.shape[2]

    def advance(turn, accum):
        start_slot = (turn * group_size).astype(jnp.int32)
        return accum + block_term(block_vals, take_ids, put_ids, live_count, source, seg_count, flipped, start_slot, group_size)
    initial = jnp.zeros((seg_count, source.shape[1], width), jnp.float32)
    return lax.fori_loop(0, slot_total // group_size, advance, initial)

def reference(features, w_neigh, w_self, bias, cotangent, block_rows, block_cols, block_vals, block_count):
    rows_tile = NODE_DEV * N_COL
    cols_tile = NODE_DEV * N_ROW
    both_w = jnp.concatenate([w_neigh, w_self], axis=1)
    projected = jnp.dot(features, both_w, preferred_element_type=jnp.float32).astype(jnp.bfloat16)
    neigh = projected[:, :HID]
    own = projected[:, HID:]

    def forward_row(row_index):
        accum = jnp.zeros((TB_R, BLK, HID), jnp.float32)
        masses = jnp.zeros((TB_R, BLK), jnp.float32)
        for col_index in range(N_COL):
            values = block_vals[row_index, col_index]
            row_ids = block_rows[row_index, col_index]
            col_ids = block_cols[row_index, col_index]
            live_count = block_count[row_index, col_index]
            source = neigh[col_index * cols_tile:(col_index + 1) * cols_tile].reshape(TB_C, BLK, HID)
            accum = accum + sparse_product(values, col_ids, row_ids, live_count, source, TB_R, False)
            live_mask = (jnp.arange(NBLK, dtype=jnp.int32) < live_count).astype(jnp.float32)
            row_mass = lax.optimization_barrier(jnp.sum(values.astype(jnp.float32), axis=2)) * live_mask[:, None]
            masses = masses + jax.ops.segment_sum(row_mass, row_ids, num_segments=TB_R)
        return (accum.reshape(rows_tile, HID), masses.reshape(rows_tile))
    aggregate, degree = lax.map(forward_row, jnp.arange(N_ROW, dtype=jnp.int32))
    aggregate = aggregate.reshape(NODES, HID)
    degree = degree.reshape(NODES)
    inverse = 1.0 / (degree + 1.0)
    preact = own.astype(jnp.float32) + aggregate * inverse[:, None] + bias
    output = jax.nn.elu(preact).astype(jnp.bfloat16)
    slopes = jnp.where(preact > 0, 1.0, jnp.exp(jnp.minimum(preact, 0.0)))
    grad_pre = cotangent.astype(jnp.float32) * slopes
    grad_round = grad_pre.astype(jnp.bfloat16)
    scaled = (grad_pre * inverse[:, None]).astype(jnp.bfloat16)

    def backward_col(col_index):
        accum = jnp.zeros((TB_C, BLK, HID), jnp.float32)
        for row_index in range(N_ROW):
            values = block_vals[row_index, col_index]
            row_ids = block_rows[row_index, col_index]
            col_ids = block_cols[row_index, col_index]
            live_count = block_count[row_index, col_index]
            source = scaled[row_index * rows_tile:(row_index + 1) * rows_tile].reshape(TB_R, BLK, HID)
            accum = accum + sparse_product(values, row_ids, col_ids, live_count, source, TB_C, True)
        return accum.reshape(cols_tile, HID)
    back = lax.map(backward_col, jnp.arange(N_COL, dtype=jnp.int32)).reshape(NODES, HID).astype(jnp.bfloat16)
    factor = 1.0 / math.sqrt(NODES)
    grad_self = jnp.dot(features.T, grad_round, preferred_element_type=jnp.float32) * factor
    grad_neigh = jnp.dot(features.T, back, preferred_element_type=jnp.float32) * (32.0 * factor)
    grad_bias = lax.optimization_barrier(jnp.sum(grad_pre, axis=0)) * factor
    grad_input = jnp.dot(grad_round, w_self.T, preferred_element_type=jnp.float32) + jnp.dot(back, w_neigh.T, preferred_element_type=jnp.float32)
    return (output, grad_input.astype(jnp.bfloat16), grad_self, grad_neigh, grad_bias)
```

```python
import math

import jax
import jax.numpy as jnp
from jax import lax
from jax.experimental import pallas as pl
from jax.experimental.pallas import tpu as pltpu
from jax.sharding import PartitionSpec as P


def densify_kernel(rows_ref, cols_ref, count_ref, vals_ref, tile_ref, mass_ref, acc):
    row_blocks, col_blocks, size, _ = acc.shape

    def clear(i, carry):
        for j in range(col_blocks):
            acc[i, j] = jnp.zeros((size, size), jnp.float32)
        return carry

    lax.fori_loop(0, row_blocks, clear, 0)

    def add(s, carry):
        i = rows_ref[s]
        j = cols_ref[s]
        acc[i, j] += vals_ref[s].astype(jnp.float32)
        return carry

    lax.fori_loop(0, count_ref[0], add, 0)
    diagonal = lax.broadcasted_iota(jnp.int32, (size, size), 0) == lax.broadcasted_iota(
        jnp.int32, (size, size), 1
    )

    def finish(i, carry):
        total = jnp.zeros((size, size), jnp.float32)
        start = pl.multiple_of(i * size, size)
        for j in range(col_blocks):
            block = acc[i, j]
            total = total + block
            tile_ref[pl.ds(start, size), j * size : (j + 1) * size] = block.astype(jnp.bfloat16)
        sums = jnp.sum(total, axis=1, keepdims=True)
        as_row = jnp.sum(jnp.where(diagonal, sums, 0.0), axis=0, keepdims=True)
        mass_ref[i] = jnp.broadcast_to(as_row, (8, size))
        return carry

    lax.fori_loop(0, row_blocks, finish, 0)


def densify(values, row_ids, col_ids, live_count, row_blocks, col_blocks):
    size = values.shape[1]
    smem = pl.BlockSpec(memory_space=pltpu.SMEM)
    vmem = pl.BlockSpec(memory_space=pltpu.VMEM)
    return pl.pallas_call(
        densify_kernel,
        out_shape=(
            jax.ShapeDtypeStruct((row_blocks * size, col_blocks * size), jnp.bfloat16),
            jax.ShapeDtypeStruct((row_blocks, 8, size), jnp.float32),
        ),
        in_specs=[smem, smem, smem, vmem],
        out_specs=(vmem, vmem),
        scratch_shapes=[pltpu.VMEM((row_blocks, col_blocks, size, size), jnp.float32)],
        compiler_params=pltpu.CompilerParams(vmem_limit_bytes=40 * 1024 * 1024),
        name="densify",
    )(row_ids, col_ids, live_count, values)


def matmul(a, b, contract):
    return lax.dot_general(a, b, ((contract[0], contract[1]), ((), ())), preferred_element_type=jnp.float32)


def local(
    features, w_neigh, w_self, bias, cotangent, block_rows, block_cols, block_vals, block_count
):
    row_size = lax.axis_size("row")
    col_size = lax.axis_size("col")
    node_dev = features.shape[0]
    values = block_vals[0, 0]
    tile, mass = densify(
        values, block_rows[0, 0], block_cols[0, 0], block_count[0], col_size, row_size
    )
    to_out = [
        (r * col_size + c, c * row_size + r) for r in range(row_size) for c in range(col_size)
    ]
    to_in = [(d, s) for s, d in to_out]
    own_feat = lax.ppermute(features, ("row", "col"), to_out)
    gathered = lax.all_gather(features, "row", axis=0, tiled=True)
    part = matmul(tile, gathered, ((1,), (0,)))
    mixed = lax.psum_scatter(part, "col", scatter_dimension=0, tiled=True)
    degree = lax.psum_scatter(mass[:, 0, :], "col", scatter_dimension=0, tiled=True)[0]
    high = mixed.astype(jnp.bfloat16)
    low = (mixed - high.astype(jnp.float32)).astype(jnp.bfloat16)
    aggregate = matmul(high, w_neigh, ((1,), (0,))) + matmul(low, w_neigh, ((1,), (0,)))
    own = matmul(own_feat, w_self, ((1,), (0,))).astype(jnp.bfloat16).astype(jnp.float32)
    inverse = 1.0 / (degree + 1.0)
    preact = own + aggregate * inverse[:, None] + bias
    output = jax.nn.elu(preact).astype(jnp.bfloat16)
    slopes = jnp.where(preact > 0, 1.0, jnp.exp(jnp.minimum(preact, 0.0)))
    grad_pre = cotangent.astype(jnp.float32) * slopes
    grad_round = grad_pre.astype(jnp.bfloat16)
    scaled = (grad_pre * inverse[:, None]).astype(jnp.bfloat16)
    part_self = matmul(own_feat, grad_round, ((0,), (0,)))
    part_neigh = matmul(high, scaled, ((0,), (0,)))
    part_bias = jnp.sum(grad_pre, axis=0)
    total_self, total_neigh, total_bias = lax.psum(
        (part_self, part_neigh, part_bias), ("row", "col")
    )
    back_in = matmul(scaled, w_neigh, ((1,), (1,))).astype(jnp.bfloat16)
    self_in = matmul(grad_round, w_self, ((1,), (1,)))
    self_in = lax.ppermute(self_in, ("row", "col"), to_in)
    back_all = lax.all_gather(back_in, "col", axis=0, tiled=True)
    back_part = matmul(tile, back_all, ((0,), (0,)))
    back = lax.psum_scatter(back_part, "row", scatter_dimension=0, tiled=True)
    grad_input = (back + self_in).astype(jnp.bfloat16)
    factor = 1.0 / math.sqrt(node_dev * row_size * col_size)
    return (
        output,
        grad_input,
        total_self * factor,
        total_neigh * (32.0 * factor),
        total_bias * factor,
    )


def solution(mesh):
    in_specs = (
        P(("col", "row"), None),
        P(),
        P(),
        P(),
        P(("row", "col"), None),
        P("row", "col", None),
        P("row", "col", None),
        P("row", "col", None, None, None),
        P("row", "col"),
    )
    out_specs = (P(("row", "col"), None), P(("col", "row"), None), P(), P(), P())
    return jax.shard_map(local, mesh=mesh, in_specs=in_specs, out_specs=out_specs, check_vma=False)
```

```python
import math

import jax
import jax.numpy as jnp
from jax import lax
from jax.experimental import pallas as pl
from jax.experimental.pallas import tpu as pltpu
from jax.sharding import PartitionSpec as P


def densify_kernel(rows_ref, cols_ref, count_ref, vals_ref, tile_ref, mass_ref, acc):
    row_blocks, col_blocks, size, _ = acc.shape

    def clear(i, carry):
        for j in range(col_blocks):
            acc[i, j] = jnp.zeros((size, size), jnp.float32)
        return carry

    lax.fori_loop(0, row_blocks, clear, 0)

    def add(s, carry):
        i = rows_ref[s]
        j = cols_ref[s]
        acc[i, j] += vals_ref[s].astype(jnp.float32)
        return carry

    lax.fori_loop(0, count_ref[0], add, 0)
    diagonal = lax.broadcasted_iota(jnp.int32, (size, size), 0) == lax.broadcasted_iota(
        jnp.int32, (size, size), 1
    )

    def finish(i, carry):
        total = jnp.zeros((size, size), jnp.float32)
        start = pl.multiple_of(i * size, size)
        for j in range(col_blocks):
            block = acc[i, j]
            total = total + block
            tile_ref[pl.ds(start, size), j * size : (j + 1) * size] = block.astype(jnp.bfloat16)
        sums = jnp.sum(total, axis=1, keepdims=True)
        as_row = jnp.sum(jnp.where(diagonal, sums, 0.0), axis=0, keepdims=True)
        mass_ref[i] = jnp.broadcast_to(as_row, (8, size))
        return carry

    lax.fori_loop(0, row_blocks, finish, 0)


def densify(values, row_ids, col_ids, live_count, row_blocks, col_blocks):
    size = values.shape[1]
    smem = pl.BlockSpec(memory_space=pltpu.SMEM)
    vmem = pl.BlockSpec(memory_space=pltpu.VMEM)
    return pl.pallas_call(
        densify_kernel,
        out_shape=(
            jax.ShapeDtypeStruct((row_blocks * size, col_blocks * size), jnp.bfloat16),
            jax.ShapeDtypeStruct((row_blocks, 8, size), jnp.float32),
        ),
        in_specs=[smem, smem, smem, vmem],
        out_specs=(vmem, vmem),
        scratch_shapes=[pltpu.VMEM((row_blocks, col_blocks, size, size), jnp.float32)],
        compiler_params=pltpu.CompilerParams(vmem_limit_bytes=40 * 1024 * 1024),
        name="densify",
    )(row_ids, col_ids, live_count, values)


MESH = pl.DeviceIdType.MESH
BF = jnp.bfloat16
F32 = jnp.float32


def remote(src, dst, send, recv, device):
    return pltpu.make_async_remote_copy(
        src_ref=src, dst_ref=dst, send_sem=send, recv_sem=recv, device_id=device, device_id_type=MESH
    )


def layer_kernel(
    tile_hbm, mass, features, wn_hbm, ws_hbm, bias, cotangent,
    out_ref, gin_ref, gself_ref, gneigh_ref, gbias_ref,
    tile, wn, ws, local_sem,
    fg, acc, own_feat, send_blocks, recv_blocks, recv_mass, mixed,
    scaled, grounded, sgt, tblock, trecv,
    x_mine, y_mine, x_other, y_other, other, other_recv, partial,
    r1, q1, r2, q2, r3, result, result2,
    halves, pair_recv, row_send, row_recv,
    bsum, bx, by, bz, bk,
    ag_s, ag_r, fw_s, fw_r, pm_s, pm_r, rs_s, rs_r, ms_s, ms_r, sg_s, sg_r, t_s, t_r,
    ot_s, ot_r, a1_s, a1_r, a2_s, a2_r, a3_s, a3_r, g3_s, g3_r, g2_s, g2_r, g1_s, g1_r, fin_s, fin_r,
    b_s, b_r, pd_s, pd_r, br_s, br_r,
):
    r = lax.axis_index("row")
    c = lax.axis_index("col")
    xl, z, core = r // 8, (r // 2) % 4, r % 2
    y, xh = c // 2, c % 2
    x = xh * 2 + xl

    def at_row(chip, k):
        return (chip * 2 + k, c)

    def chip_fwd(k):
        return ((xl + k // 4) % 2) * 4 + (z + k) % 4

    def chip_back(k):
        return ((xl + 2 - k // 4) % 2) * 4 + (z + 8 - k) % 4

    def device_of(px, py, pz):
        return (((px % 2) * 4 + pz) * 2 + core, py * 2 + px // 2)

    here = (x, y, z)
    axis_orders = ((0, 1, 2), (1, 2, 0), (2, 0, 1))

    def along(axis, d):
        spot = list(here)
        spot[axis] = (spot[axis] + d) % 4
        return device_of(*spot)

    partner = (r + 1 - 2 * core, c)
    node = c * 16 + r
    out_dev = (node // 8, node % 8)
    block = r * 8 + c
    in_dev = (block % 16, block // 16)
    moved = node != block

    copies = [
        pltpu.make_async_copy(tile_hbm, tile, local_sem.at[0]),
        pltpu.make_async_copy(ws_hbm, ws, local_sem.at[1]),
        pltpu.make_async_copy(wn_hbm, wn, local_sem.at[2]),
    ]
    for copy in copies:
        copy.start()

    barrier = pltpu.get_barrier_semaphore()

    def hello(device):
        pl.semaphore_signal(barrier, inc=1, device_id=device, device_id_type=MESH)

    def hello_row(k, carry):
        hello(at_row(chip_fwd(k), core))
        return carry

    def hello_col(k, carry):
        hello((r, (c + k) % 8))
        return carry

    lax.fori_loop(1, 8, hello_row, 0)
    lax.fori_loop(1, 8, hello_col, 0)
    hello(partner)
    hello((((1 - xl) * 4 + z) * 2 + core, y * 2 + 1 - xh))

    @pl.when(moved)
    def _():
        hello(out_dev)
        hello(in_dev)
        pl.semaphore_wait(barrier, 18)

    @pl.when(jnp.logical_not(moved))
    def _():
        pl.semaphore_wait(barrier, 16)

    def gather_send(k):
        return remote(
            features, fg.at[pl.ds(r * 128, 128)], ag_s.at[k], ag_r.at[k], at_row(chip_fwd(k), core)
        )

    def gather_recv(k):
        rows = pl.ds((chip_back(k) * 2 + core) * 128, 128)
        return remote(features, fg.at[rows], ag_s.at[k], ag_r.at[k], at_row(chip_back(k), core))

    def forward(k):
        rows = pl.ds((chip_back(k) * 2 + core) * 128, 128)
        return remote(fg.at[rows], fg.at[rows], fw_s.at[k], fw_r.at[k], partner)

    def forward_recv(k):
        rows = pl.ds((chip_back(k) * 2 + 1 - core) * 128, 128)
        return remote(fg.at[rows], fg.at[rows], fw_s.at[k], fw_r.at[k], partner)

    def permute():
        return remote(features, own_feat, pm_s.at[0], pm_r.at[0], out_dev)

    def mass_send(k):
        to = (c + k) % 8
        return remote(mass.at[to], recv_mass.at[k - 1], ms_s.at[k], ms_r.at[k], (r, to))

    def start_gather(k, carry):
        gather_send(k).start()
        return carry

    lax.fori_loop(1, 8, start_gather, 0)

    @pl.when(moved)
    def _():
        permute().start()

    @pl.when(jnp.logical_not(moved))
    def _():
        own_feat[...] = features[...]

    def start_mass(k, carry):
        mass_send(k).start()
        return carry

    lax.fori_loop(1, 8, start_mass, 0)
    fg[pl.ds(r * 128, 128), :] = features[...]

    def clear(i, carry):
        acc[pl.ds(i * 128, 128), :] = jnp.zeros((128, 768), F32)
        return carry

    lax.fori_loop(0, 8, clear, 0)
    copies[0].wait()

    def gather_step(k, carry):
        @pl.when(k > 0)
        def _():
            gather_recv(k).wait_recv()

        forward(k).start()
        forward_recv(k).wait_recv()
        return carry

    def product(rows, k):
        where = pl.ds(pl.multiple_of(chip_back(k) * 256, 256), 256)
        return jnp.dot(tile[rows, where], fg[where, :], preferred_element_type=F32)

    def mix_step(k, carry):
        gather_step(k, 0)

        def rows_step(m, inner):
            rows = pl.ds(pl.multiple_of(m * 512, 512), 512)
            acc[rows, :] += product(rows, k)
            return inner

        return lax.fori_loop(0, 2, rows_step, carry)

    lax.fori_loop(0, 7, mix_step, 0)
    gather_step(7, 0)

    def reduce_send(k):
        to = (c + k) % 8
        return remote(send_blocks.at[to], recv_blocks.at[k - 1], rs_s.at[k], rs_r.at[k], (r, to))

    def reduce_step(k, carry):
        to = (c + k) % 8
        rows = pl.ds(pl.multiple_of(to * 128, 128), 128)
        send_blocks[to] = (acc[rows, :] + product(rows, 7)).astype(BF)
        reduce_send(k).start()
        return carry

    lax.fori_loop(1, 8, reduce_step, 0)
    mine = pl.ds(pl.multiple_of(c * 128, 128), 128)
    mixed[...] = acc[mine, :] + product(mine, 7)

    copies[1].wait()
    copies[2].wait()

    @pl.when(moved)
    def _():
        permute().wait_recv()

    def mass_step(k, total):
        mass_send(k).wait_recv()
        return total + recv_mass[k - 1]

    degree = lax.fori_loop(1, 8, mass_step, mass[c])

    def sum_step(k, carry):
        reduce_send(k).wait_recv()
        mixed[...] += recv_blocks[k - 1].astype(F32)
        return carry

    lax.fori_loop(1, 8, sum_step, 0)

    diagonal = lax.broadcasted_iota(jnp.int32, (128, 128), 0) == lax.broadcasted_iota(
        jnp.int32, (128, 128), 1
    )
    column = jnp.sum(jnp.where(diagonal, degree[0:1, :], 0.0), axis=1, keepdims=True)
    inverse = 1.0 / (column + 1.0)
    high = mixed[...].astype(BF)
    low = (mixed[...] - high.astype(F32)).astype(BF)
    mixed_high = x_other
    mixed_high[...] = high
    x_mine[...] = low

    def layer_step(n, carry):
        cols = pl.ds(pl.multiple_of(n * 256, 256), 256)
        aggregate = jnp.dot(mixed_high[...], wn[:, cols], preferred_element_type=F32)
        aggregate += jnp.dot(x_mine[...], wn[:, cols], preferred_element_type=F32)
        own = jnp.dot(own_feat[...], ws[:, cols], preferred_element_type=F32)
        preact = own.astype(BF).astype(F32) + aggregate * inverse + bias[:, cols]
        small = jnp.exp(jnp.minimum(preact, 0.0))
        above = preact > 0
        out_ref[:, cols] = jnp.where(above, preact, small - 1.0).astype(BF)
        grad = cotangent[:, cols].astype(F32) * jnp.where(above, 1.0, small)
        grounded[:, cols] = grad.astype(BF)
        scaled[:, cols] = (grad * inverse).astype(BF)
        bsum[:, cols] = jnp.sum(grad, axis=0, keepdims=True)
        return carry

    lax.fori_loop(0, 4, layer_step, 0)

    lanes = pl.ds(pl.multiple_of(c * 128, 128), 128)
    turned = (((1,), (1,)), ((), ()))
    sgt[:, lanes] = lax.dot_general(
        wn[...], scaled[...], turned, preferred_element_type=F32
    ).astype(BF)

    def spread_send(k):
        return remote(sgt.at[:, lanes], sgt.at[:, lanes], sg_s.at[k], sg_r.at[k], (r, (c + k) % 8))

    def spread_recv(k):
        source = pl.ds(pl.multiple_of(((c + 8 - k) % 8) * 128, 128), 128)
        return remote(sgt.at[:, source], sgt.at[:, source], sg_s.at[k], sg_r.at[k], (r, (c + k) % 8))

    def start_spread(k, carry):
        spread_send(k).start()
        return carry

    lax.fori_loop(1, 8, start_spread, 0)
    tblock[...] = lax.dot_general(
        ws[...], grounded[...], turned, preferred_element_type=F32
    ).astype(BF)

    def self_send():
        return remote(tblock, trecv, t_s.at[0], t_r.at[0], in_dev)

    @pl.when(moved)
    def _():
        self_send().start()

    @pl.when(jnp.logical_not(moved))
    def _():
        trecv[...] = tblock[...]

    @pl.when(core == 0)
    def _():
        x_mine[...] = own_feat[...]
        y_mine[...] = grounded[...]
        y_other[...] = scaled[...]

    @pl.when(core == 1)
    def _():
        x_mine[...] = x_other[...]
        x_other[...] = own_feat[...]
        y_mine[...] = scaled[...]
        y_other[...] = grounded[...]

    flipped = (((0,), (0,)), ((), ()))

    def part(j):
        return pl.ds(j * 256, 256)

    def other_send(j):
        return remote(other.at[part(j)], other_recv.at[part(j)], ot_s.at[j], ot_r.at[j], partner)

    for j in range(3):
        other[part(j), :] = lax.dot_general(
            x_other[:, part(j)], y_other[...], flipped, preferred_element_type=F32
        ).astype(BF)
        other_send(j).start()

    def stage1(j, d):
        axis = axis_orders[j][0]
        rows = pl.ds(pl.multiple_of(j * 256 + ((here[axis] + d) % 4) * 64, 64), 64)
        n = j * 3 + d - 1
        return remote(partial.at[rows], r1.at[n], a1_s.at[n], a1_r.at[n], along(axis, d))

    for j in range(3):
        mine_part = lax.dot_general(
            x_mine[:, part(j)], y_mine[...], flipped, preferred_element_type=F32
        )
        other_send(j).wait_recv()
        partial[part(j), :] = (mine_part + other_recv[part(j), :].astype(F32)).astype(BF)
        for d in range(1, 4):
            stage1(j, d).start()

    bias_slots = (bx, by, bz)

    def bias_send(axis, d):
        n = axis * 3 + d - 1
        slot = bias_slots[axis].at[here[axis]]
        return remote(slot, slot, b_s.at[n], b_r.at[n], along(axis, d))

    def bias_recv(axis, d):
        n = axis * 3 + d - 1
        slot = bias_slots[axis].at[(here[axis] + 4 - d) % 4]
        return remote(slot, slot, b_s.at[n], b_r.at[n], along(axis, d))

    def bias_start(axis, value):
        bias_slots[axis][here[axis]] = value
        for d in range(1, 4):
            bias_send(axis, d).start()

    def bias_total(axis):
        for d in range(1, 4):
            bias_recv(axis, d).wait_recv()
        slots = bias_slots[axis]
        return (slots[0] + slots[1]) + (slots[2] + slots[3])

    bias_start(0, jnp.concatenate([bsum[:, i * 128 : (i + 1) * 128] for i in range(8)], axis=0))

    def wait_spread(k, carry):
        spread_recv(k).wait_recv()
        return carry

    lax.fori_loop(1, 8, wait_spread, 0)

    def pair_send(k):
        return remote(halves.at[k, 1 - core], pair_recv.at[k], pd_s.at[k], pd_r.at[k], partner)

    def row_out(k):
        return remote(
            row_send.at[k], row_recv.at[k - 1], br_s.at[k], br_r.at[k], at_row(chip_fwd(k), core)
        )

    def pair_sum(k):
        pair_send(k).wait_recv()
        return halves[k, core].astype(F32) + pair_recv[k].astype(F32)

    def back_step(t, carry):
        k = (t + 1) % 8
        where = pl.ds(pl.multiple_of(chip_fwd(k) * 256, 256), 256)
        value = jnp.dot(sgt[...], tile[:, where], preferred_element_type=F32)
        halves[k, 0] = value[:, :128].astype(BF)
        halves[k, 1] = value[:, 128:].astype(BF)
        pair_send(k).start()

        @pl.when(t > 0)
        def _():
            row_send[t] = pair_sum(t).astype(BF)
            row_out(t).start()

        return carry

    lax.fori_loop(0, 8, back_step, 0)

    def stage2(j, d):
        axis = axis_orders[j][1]
        rows = pl.ds(pl.multiple_of(((here[axis] + d) % 4) * 16, 16), 16)
        n = j * 3 + d - 1
        return remote(q1.at[j, rows], r2.at[n], a2_s.at[n], a2_r.at[n], along(axis, d))

    def stage3(j, d):
        axis = axis_orders[j][2]
        cols = pl.ds(pl.multiple_of(((here[axis] + d) % 4) * 256, 256), 256)
        n = j * 3 + d - 1
        return remote(q2.at[j, :, cols], r3.at[n], a3_s.at[n], a3_r.at[n], along(axis, d))

    for j in range(3):
        axis = axis_orders[j][0]
        for d in range(1, 4):
            stage1(j, d).wait_recv()
        rows = pl.ds(pl.multiple_of(j * 256 + here[axis] * 64, 64), 64)
        total = partial[rows, :].astype(F32)
        for d in range(3):
            total = total + r1[j * 3 + d].astype(F32)
        q1[j] = total
        for d in range(1, 4):
            stage2(j, d).start()
    bias_start(1, bias_total(0))
    for j in range(3):
        axis = axis_orders[j][1]
        for d in range(1, 4):
            stage2(j, d).wait_recv()
        total = q1[j, pl.ds(pl.multiple_of(here[axis] * 16, 16), 16), :]
        for d in range(3):
            total = total + r2[j * 3 + d]
        q2[j] = total
        for d in range(1, 4):
            stage3(j, d).start()
    bias_start(2, bias_total(1))

    def place(j, shift, axis_step):
        a, b, e = axis_orders[j]
        spot = list(here)
        moving = axis_orders[j][axis_step]
        spot[moving] = (spot[moving] + 4 - shift) % 4
        start = j * 256 + spot[a] * 64
        if axis_step == 0:
            return result.at[pl.ds(pl.multiple_of(start, 64), 64)]
        rows = pl.ds(pl.multiple_of(start + spot[b] * 16, 16), 16)
        if axis_step == 1:
            return result.at[rows]
        return result.at[rows, pl.ds(pl.multiple_of(spot[e] * 256, 256), 256)]

    def back_copy(j, d, axis_step, shift, sends, recvs):
        n = j * 3 + d - 1
        ref = place(j, shift, axis_step)
        return remote(ref, ref, sends.at[n], recvs.at[n], along(axis_orders[j][axis_step], d))

    for j in range(3):
        axis = axis_orders[j][2]
        for d in range(1, 4):
            stage3(j, d).wait_recv()
        cols = pl.ds(pl.multiple_of(here[axis] * 256, 256), 256)
        total = q2[j, :, cols]
        for d in range(3):
            total = total + r3[j * 3 + d]
        place(j, 0, 2)[...] = total.astype(BF)
        for d in range(1, 4):
            back_copy(j, d, 2, 0, g3_s, g3_r).start()
    bias_core = bias_total(2)
    bk[core] = bias_core

    def bias_pair(slot):
        return remote(bk.at[slot], bk.at[slot], b_s.at[9], b_r.at[9], partner)

    bias_pair(core).start()
    for j in range(3):
        for d in range(1, 4):
            back_copy(j, d, 2, d, g3_s, g3_r).wait_recv()
        for d in range(1, 4):
            back_copy(j, d, 1, 0, g2_s, g2_r).start()
    for j in range(3):
        for d in range(1, 4):
            back_copy(j, d, 1, d, g2_s, g2_r).wait_recv()
        for d in range(1, 4):
            back_copy(j, d, 0, 0, g1_s, g1_r).start()

    def finish_copy(j, d, shifted):
        n = j * 4 + d
        axis = axis_orders[j][0]
        spot = (here[axis] + 4 - d) % 4
        rows = pl.ds(pl.multiple_of(j * 256 + spot * 64, 64), 64)
        return remote(result.at[rows], result2.at[rows], fin_s.at[n], fin_r.at[n], partner)

    for j in range(3):
        finish_copy(j, 0, 0).start()

    def row_total(k, total):
        row_out(k).wait_recv()
        return total + row_recv[k - 1].astype(F32)

    @pl.when(moved)
    def _():
        self_send().wait_recv()

    total = pair_sum(0) + trecv[...].astype(F32)
    total = lax.fori_loop(1, 8, row_total, total)
    gin_ref[...] = total.T.astype(BF)

    for j in range(3):
        for d in range(1, 4):
            back_copy(j, d, 0, d, g1_s, g1_r).wait_recv()
            finish_copy(j, d, 0).start()
    bias_pair(1 - core).wait_recv()
    gbias_ref[...] = bk[0] + bk[1]
    for j in range(3):
        for d in range(4):
            finish_copy(j, d, 0).wait_recv()

    @pl.when(core == 0)
    def _():
        gself_ref[...] = result[...]
        gneigh_ref[...] = result2[...]

    @pl.when(core == 1)
    def _():
        gself_ref[...] = result2[...]
        gneigh_ref[...] = result[...]

    def drain(k, carry):
        gather_send(k).wait_send()
        mass_send(k).wait_send()
        reduce_send(k).wait_send()
        spread_send(k).wait_send()
        row_out(k).wait_send()
        return carry

    lax.fori_loop(1, 8, drain, 0)

    def drain_pairs(k, carry):
        forward(k).wait_send()
        pair_send(k).wait_send()
        return carry

    lax.fori_loop(0, 8, drain_pairs, 0)

    @pl.when(moved)
    def _():
        permute().wait_send()
        self_send().wait_send()

    for j in range(3):
        other_send(j).wait_send()
        for d in range(1, 4):
            stage1(j, d).wait_send()
            stage2(j, d).wait_send()
            stage3(j, d).wait_send()
            back_copy(j, d, 2, 0, g3_s, g3_r).wait_send()
            back_copy(j, d, 1, 0, g2_s, g2_r).wait_send()
            back_copy(j, d, 0, 0, g1_s, g1_r).wait_send()
            bias_send(j, d).wait_send()
        for d in range(4):
            finish_copy(j, d, 0).wait_send()
    bias_pair(core).wait_send()


def layer(tile, mass, features, w_neigh, w_self, bias, cotangent):
    vmem = pl.BlockSpec(memory_space=pltpu.VMEM)
    hbm = pl.BlockSpec(memory_space=pl.ANY)
    sem = pltpu.SemaphoreType.DMA
    V = pltpu.VMEM
    shape = jax.ShapeDtypeStruct
    return pl.pallas_call(
        layer_kernel,
        out_shape=(
            shape((128, 1024), BF),
            shape((128, 768), BF),
            shape((768, 1024), BF),
            shape((768, 1024), BF),
            shape((8, 128), F32),
        ),
        in_specs=[hbm, vmem, vmem, hbm, hbm, vmem, vmem],
        out_specs=(vmem,) * 5,
        scratch_shapes=[
            V((1024, 2048), BF), V((768, 1024), BF), V((768, 1024), BF), sem((3,)),
            V((2048, 768), BF), V((1024, 768), F32), V((128, 768), BF), V((8, 128, 768), BF),
            V((7, 128, 768), BF), V((7, 8, 128), F32), V((128, 768), F32),
            V((128, 1024), BF), V((128, 1024), BF), V((768, 1024), BF), V((768, 128), BF), V((768, 128), BF),
            V((128, 768), BF), V((128, 1024), BF), V((128, 768), BF), V((128, 1024), BF),
            V((768, 1024), BF), V((768, 1024), BF), V((768, 1024), BF),
            V((9, 64, 1024), BF), V((3, 64, 1024), F32), V((9, 16, 1024), F32), V((3, 16, 1024), F32),
            V((9, 16, 256), F32), V((768, 1024), BF), V((768, 1024), BF),
            V((8, 2, 768, 128), BF), V((8, 768, 128), BF), V((8, 768, 128), BF), V((7, 768, 128), BF),
            V((1, 1024), F32), V((4, 8, 128), F32), V((4, 8, 128), F32), V((4, 8, 128), F32), V((2, 8, 128), F32),
        ]
        + [sem((8,))] * 4 + [sem((1,))] * 2 + [sem((8,))] * 6 + [sem((1,))] * 2 + [sem((3,))] * 2
        + [sem((9,))] * 12 + [sem((12,))] * 2 + [sem((10,))] * 2 + [sem((8,))] * 4,
        compiler_params=pltpu.CompilerParams(
            collective_id=0, has_side_effects=True, vmem_limit_bytes=58 * 1024 * 1024
        ),
        name="layer",
    )(tile, mass, features, w_neigh, w_self, bias, cotangent)


def local(
    features, w_neigh, w_self, bias, cotangent, block_rows, block_cols, block_vals, block_count
):
    row_size = lax.axis_size("row")
    col_size = lax.axis_size("col")
    node_dev = features.shape[0]
    tile, mass = densify(
        block_vals[0, 0], block_rows[0, 0], block_cols[0, 0], block_count[0], col_size, row_size
    )
    output, grad_input, g_self, g_neigh, g_bias = layer(
        tile, mass, features, w_neigh, w_self, bias.reshape(1, -1), cotangent
    )
    factor = 1.0 / math.sqrt(node_dev * row_size * col_size)
    return (
        output,
        grad_input,
        g_self.astype(F32) * factor,
        g_neigh.astype(F32) * (32.0 * factor),
        g_bias.reshape(-1) * factor,
    )


def solution(mesh):
    in_specs = (
        P(("col", "row"), None),
        P(),
        P(),
        P(),
        P(("row", "col"), None),
        P("row", "col", None),
        P("row", "col", None),
        P("row", "col", None, None, None),
        P("row", "col"),
    )
    out_specs = (P(("row", "col"), None), P(("col", "row"), None), P(), P(), P())
    return jax.shard_map(local, mesh=mesh, in_specs=in_specs, out_specs=out_specs, check_vma=False)
```

```python
import functools
import math

import jax
import jax.numpy as jnp
from jax import lax
from jax.experimental import pallas as pl
from jax.experimental.pallas import tpu as pltpu
from jax.sharding import PartitionSpec as P


def densify_kernel(
    rows_ref, cols_ref, count_ref, vals_hbm, tile_hbm, mass_ref, vals, acc, tile, in_sem, out_sem
):
    row_blocks, col_blocks, size, _ = acc.shape
    pieces = 4
    span = vals.shape[0] // pieces

    def load(q):
        slots = pl.ds(q * span, span)
        return pltpu.make_async_copy(vals_hbm.at[slots], vals.at[slots], in_sem.at[q])

    def store(i):
        rows = pl.ds(pl.multiple_of(i * size, size), size)
        return pltpu.make_async_copy(tile.at[rows], tile_hbm.at[rows], out_sem.at[i])

    for q in range(pieces):
        load(q).start()

    def clear(i, carry):
        for j in range(col_blocks):
            acc[i, j] = jnp.zeros((size, size), jnp.float32)
        return carry

    lax.fori_loop(0, row_blocks, clear, 0)

    def add(s, carry):
        i = rows_ref[s]
        j = cols_ref[s]
        acc[i, j] += vals[s].astype(jnp.float32)
        return carry

    count = count_ref[0]
    for q in range(pieces):
        load(q).wait()
        lax.fori_loop(q * span, jnp.minimum(count, (q + 1) * span), add, 0)
    diagonal = lax.broadcasted_iota(jnp.int32, (size, size), 0) == lax.broadcasted_iota(
        jnp.int32, (size, size), 1
    )

    def finish(i, carry):
        total = jnp.zeros((size, size), jnp.float32)
        start = pl.multiple_of(i * size, size)
        for j in range(col_blocks):
            block = acc[i, j]
            total = total + block
            tile[pl.ds(start, size), j * size : (j + 1) * size] = block.astype(jnp.bfloat16)
        store(i).start()
        sums = jnp.sum(total, axis=1, keepdims=True)
        as_row = jnp.sum(jnp.where(diagonal, sums, 0.0), axis=0, keepdims=True)
        mass_ref[i] = jnp.broadcast_to(as_row, (8, size))
        return carry

    lax.fori_loop(0, row_blocks, finish, 0)
    for i in range(row_blocks):
        store(i).wait()


def densify(values, row_ids, col_ids, live_count, row_blocks, col_blocks):
    slots, size, _ = values.shape
    smem = pl.BlockSpec(memory_space=pltpu.SMEM)
    hbm = pl.BlockSpec(memory_space=pl.ANY)
    vmem = pl.BlockSpec(memory_space=pltpu.VMEM)
    rows, cols = row_blocks * size, col_blocks * size
    return pl.pallas_call(
        densify_kernel,
        out_shape=(
            jax.ShapeDtypeStruct((rows, cols), jnp.bfloat16),
            jax.ShapeDtypeStruct((row_blocks, 8, size), jnp.float32),
        ),
        in_specs=[smem, smem, smem, hbm],
        out_specs=(hbm, vmem),
        scratch_shapes=[
            pltpu.VMEM((slots, size, size), jnp.bfloat16),
            pltpu.VMEM((row_blocks, col_blocks, size, size), jnp.float32),
            pltpu.VMEM((rows, cols), jnp.bfloat16),
            pltpu.SemaphoreType.DMA((4,)),
            pltpu.SemaphoreType.DMA((row_blocks,)),
        ],
        compiler_params=pltpu.CompilerParams(vmem_limit_bytes=60 * 1024 * 1024),
        name="densify",
    )(row_ids, col_ids, live_count, values)


def finish_kernel(
    own_scale, neigh_scale, g_hbm, out_in, gin_in, bias_in,
    own_to, neigh_to, out_to, gin_to, bias_to, held, wide, in_sem, out_sem,
):
    pieces = in_sem.shape[0]
    rows = g_hbm.shape[1]
    step = 2 * rows // pieces
    loads = []
    stores = []
    for p in range(pieces):
        which, at = p % 2, pl.ds(p // 2 * step, step)
        target = (own_to, neigh_to)[which]
        loads.append(pltpu.make_async_copy(g_hbm.at[which, at], held.at[which, at], in_sem.at[p]))
        stores.append(pltpu.make_async_copy(wide.at[which, at], target.at[at], out_sem.at[p]))
    for load in loads:
        load.start()
    out_to[...] = out_in[...]
    gin_to[...] = gin_in[...]
    bias_to[...] = bias_in[...] * own_scale
    for p in range(pieces):
        which, at = p % 2, pl.ds(p // 2 * step, step)
        loads[p].wait()
        wide[which, at] = held[which, at].astype(jnp.float32) * (own_scale, neigh_scale)[which]
        stores[p].start()
    for copy in stores:
        copy.wait()


def finish(grads, output, grad_input, g_bias, own_scale, neigh_scale):
    _, rows, cols = grads.shape
    hbm = pl.BlockSpec(memory_space=pl.ANY)
    vmem = pl.BlockSpec(memory_space=pltpu.VMEM)
    shape = jax.ShapeDtypeStruct
    wide = shape((rows, cols), jnp.float32)
    pieces = 12
    return pl.pallas_call(
        functools.partial(finish_kernel, own_scale, neigh_scale),
        out_shape=(
            wide,
            wide,
            shape(output.shape, output.dtype),
            shape(grad_input.shape, grad_input.dtype),
            shape(g_bias.shape, g_bias.dtype),
        ),
        in_specs=[hbm, vmem, vmem, vmem],
        out_specs=(hbm, hbm, vmem, vmem, vmem),
        scratch_shapes=[
            pltpu.VMEM((2, rows, cols), jnp.bfloat16),
            pltpu.VMEM((2, rows, cols), jnp.float32),
            pltpu.SemaphoreType.DMA((pieces,)),
            pltpu.SemaphoreType.DMA((pieces,)),
        ],
        compiler_params=pltpu.CompilerParams(vmem_limit_bytes=60 * 1024 * 1024),
        name="finish",
    )(grads, output, grad_input, g_bias)


MESH = pl.DeviceIdType.MESH
BF = jnp.bfloat16
F32 = jnp.float32


def remote(src, dst, send, recv, device):
    return pltpu.make_async_remote_copy(
        src_ref=src, dst_ref=dst, send_sem=send, recv_sem=recv, device_id=device, device_id_type=MESH
    )


def layer_kernel(
    tile_hbm, mass, features, wn_hbm, ws_hbm, bias, cotangent,
    out_ref, gin_ref, g_ref, gbias_ref,
    tile, wn, ws, local_sem,
    fg, own_feat, send_blocks, recv_blocks, cross_send, cross_recv,
    mass_recv, mass_cross, mass_sum, mixed, group,
    scaled, grounded, sgt, tblock, trecv,
    x_mine, y_mine, x_other, y_other, other, other_recv, partial,
    r1, q1, r2, q2, r3, result, result2,
    halves, pair_recv, row_send, row_recv, row_group, side_send, side_recv,
    bsum, bx, by, bz, bk,
    gx_s, gx_r, gz_s, gz_r, fw_s, fw_r, pm_s, pm_r, ms_s, ms_r, rs_s, rs_r, rx_s, rx_r,
    sx_s, sx_r, sy_s, sy_r, t_s, t_r,
    ot_s, ot_r, a1_s, a1_r, a2_s, a2_r, a3_s, a3_r, g3_s, g3_r, g2_s, g2_r, g1_s, g1_r, fin_s, fin_r,
    b_s, b_r, pd_s, pd_r, rz_s, rz_r, rl_s, rl_r, w1_sem, w2_sem,
):
    r = lax.axis_index("row")
    c = lax.axis_index("col")
    xl, z, core = r // 8, (r // 2) % 4, r % 2
    y, xh = c // 2, c % 2
    x = xh * 2 + xl

    def device_of(px, py, pz):
        return (((px % 2) * 4 + pz) * 2 + core, py * 2 + px // 2)

    here = (x, y, z)
    axis_orders = ((0, 1, 2), (1, 2, 0), (2, 0, 1))

    def along(axis, d):
        spot = list(here)
        spot[axis] = (spot[axis] + d) % 4
        return device_of(*spot)

    partner = (r + 1 - 2 * core, c)
    here_id = r * 8 + c
    block = r * 8 + c
    first, first_col = block % 16, block // 16

    def target(d):
        from_row = (xl * 4 + (z + 4 - d) % 4) * 2 + core
        node = c * 16 + from_row
        return node // 8, node % 8

    def holder(d):
        chip = first // 8 * 4 + (first // 2 + d) % 4
        return chip * 2 + first % 2, first_col

    def is_here(device):
        return device[0] * 8 + device[1] == here_id

    copies = [
        pltpu.make_async_copy(tile_hbm, tile, local_sem.at[0]),
        pltpu.make_async_copy(ws_hbm, ws, local_sem.at[1]),
        pltpu.make_async_copy(wn_hbm, wn, local_sem.at[2]),
    ]
    for copy in copies:
        copy.start()

    barrier = pltpu.get_barrier_semaphore()

    def hello(device):
        pl.semaphore_signal(barrier, inc=1, device_id=device, device_id_type=MESH)

    x_side = (((1 - xl) * 4 + z) * 2 + core, c)
    far_side = (r, y * 2 + 1 - xh)

    def z_peer(d):
        return ((xl * 4 + (z + d) % 4) * 2 + core, c)

    def y_peer(d):
        return (r, ((y + d) % 4) * 2 + xh)

    for d in range(1, 4):
        hello(z_peer(d))
        hello(y_peer(d))
    hello(x_side)
    hello(far_side)
    hello(partner)
    hello((((1 - xl) * 4 + z) * 2 + core, y * 2 + 1 - xh))

    remote_peers = 10
    for d in range(4):
        for device in (target(d), holder(d)):
            away = jnp.logical_not(is_here(device))
            remote_peers = remote_peers + away.astype(jnp.int32)

            @pl.when(away)
            def _():
                hello(device)

    pl.semaphore_wait(barrier, remote_peers)

    for n in range(3):
        fg[n, pl.ds(r * 128, 128), :] = features[:, n * 256 : (n + 1) * 256]

    def source_rows_start(s, d, k):
        chip = ((xl + s) % 2) * 4 + (z + 4 - d) % 4
        return (chip * 2 + k) * 128

    def source_rows(s, d, k):
        return pl.ds(pl.multiple_of(source_rows_start(s, d, k), 128), 128)

    def side_gather(n):
        ref = fg.at[n, source_rows(0, 0, core)]
        return remote(ref, ref, gx_s.at[n], gx_r.at[n], x_side)

    def gather_send(n, s, d):
        m = (n * 2 + s) * 4 + d
        ref = fg.at[n, source_rows(s, 0, core)]
        return remote(ref, ref, gz_s.at[m], gz_r.at[m], z_peer(d))

    def gather_recv(n, s, d):
        m = (n * 2 + s) * 4 + d
        ref = fg.at[n, source_rows(s, d, core)]
        return remote(ref, ref, gz_s.at[m], gz_r.at[m], z_peer(d))

    def forward(n, s, d):
        m = (n * 2 + s) * 4 + d
        ref = fg.at[n, source_rows(s, d, core)]
        return remote(ref, ref, fw_s.at[m], fw_r.at[m], partner)

    def own_piece(n, d):
        return own_feat.at[n, pl.ds(d * 32, 32)]

    def permute(n, d):
        start = source_rows_start(0, d, core) + d * 32
        rows = pl.ds(pl.multiple_of(start, 32), 32)
        m = d * 3 + n
        return remote(fg.at[n, rows], own_piece(n, d), pm_s.at[m], pm_r.at[m], target(d))

    def permute_start(n):
        for d in range(4):

            @pl.when(jnp.logical_not(is_here(target(d))))
            def _():
                permute(n, d).start()

            @pl.when(is_here(target(d)))
            def _():
                start = source_rows_start(0, d, core) + d * 32
                own_feat[n, d * 32 : (d + 1) * 32, :] = fg[n, pl.ds(pl.multiple_of(start, 32), 32), :]

    def permute_wait(n):
        for d in range(4):

            @pl.when(jnp.logical_not(is_here(holder(d))))
            def _():
                permute(n, d).wait_recv()

    def mass_send(d):
        to = ((y + d) % 4) * 2
        return remote(mass.at[pl.ds(to, 2)], mass_recv.at[d - 1], ms_s.at[d], ms_r.at[d], y_peer(d))

    def mass_side():
        return remote(mass_sum.at[1 - xh], mass_cross, ms_s.at[0], ms_r.at[0], far_side)

    def spread_gather(n):
        side_gather(n).wait_recv()
        for s in range(2):
            for d in range(1, 4):
                gather_send(n, s, d).start()

    for n in range(3):
        side_gather(n).start()
    for d in range(1, 4):
        gather_send(0, 0, d).start()
    for d in range(1, 4):
        mass_send(d).start()
    side_gather(0).wait_recv()
    for d in range(1, 4):
        gather_send(0, 1, d).start()
    spread_gather(1)

    copies[0].wait()

    def reduce_send(n, d):
        m = n * 4 + d
        return remote(
            send_blocks.at[n, d], recv_blocks.at[n, d - 1], rs_s.at[m], rs_r.at[m], y_peer(d)
        )

    def cross(n):
        return remote(cross_send.at[n], cross_recv.at[n], rx_s.at[n], rx_r.at[n], far_side)

    def mix(n):
        for s in range(2):
            forward(n, s, 0).start()
        for s in range(2):
            for d in range(1, 4):
                gather_recv(n, s, d).wait_recv()
                forward(n, s, d).start()
        if n == 0:
            spread_gather(2)
        for s in range(2):
            for d in range(4):
                forward(n, s, d).wait_recv()

        def mix_step(t, carry):
            d = (t + 1) % 4
            rows = pl.ds(pl.multiple_of(((y + d) % 4) * 256, 256), 256)
            value = jnp.dot(tile[rows, :], fg[n], preferred_element_type=F32)

            @pl.when(t < 3)
            def _():
                send_blocks[n, d] = value.astype(BF)
                reduce_send(n, d).start()

            @pl.when(t == 3)
            def _():
                group[n, 0] = value[:128]
                group[n, 1] = value[128:]

            return carry

        lax.fori_loop(0, 4, mix_step, 0)

    def cross_start(n):
        for d in range(1, 4):
            reduce_send(n, d).wait_recv()
        for h in range(2):
            total = group[n, h]
            for d in range(3):
                total = total + recv_blocks[n, d, h * 128 : (h + 1) * 128].astype(F32)
            group[n, h] = total
        cross_send[n] = group[n, 1 - xh].astype(BF)
        cross(n).start()

    mix(0)
    permute_start(0)
    mix(1)
    permute_start(1)
    cross_start(0)
    for d in range(1, 4):
        mass_send(d).wait_recv()
    for h in range(2):
        mass_sum[h] = mass[y * 2 + h] + ((mass_recv[0, h] + mass_recv[1, h]) + mass_recv[2, h])
    mass_side().start()
    mix(2)
    permute_start(2)
    cross_start(1)
    cross_start(2)
    copies[1].wait()
    copies[2].wait()

    for n in range(3):
        permute_wait(n)
    mass_side().wait_recv()
    degree = mass_sum[xh] + mass_cross[...]
    for n in range(3):
        cross(n).wait_recv()
        mixed[:, n * 256 : (n + 1) * 256] = group[n, xh] + cross_recv[n].astype(F32)

    diagonal = lax.broadcasted_iota(jnp.int32, (128, 128), 0) == lax.broadcasted_iota(
        jnp.int32, (128, 128), 1
    )
    column = jnp.sum(jnp.where(diagonal, degree[0:1, :], 0.0), axis=1, keepdims=True)
    inverse = 1.0 / (column + 1.0)
    high = mixed[...].astype(BF)
    low = (mixed[...] - high.astype(F32)).astype(BF)
    mixed_high = x_other
    mixed_high[...] = high
    x_mine[...] = low

    def layer_step(n, carry):
        cols = pl.ds(pl.multiple_of(n * 256, 256), 256)
        aggregate = jnp.dot(mixed_high[...], wn[:, cols], preferred_element_type=F32)
        aggregate += jnp.dot(x_mine[...], wn[:, cols], preferred_element_type=F32)
        own = jnp.dot(own_feat[0], ws[0:256, cols], preferred_element_type=F32)
        own += jnp.dot(own_feat[1], ws[256:512, cols], preferred_element_type=F32)
        own += jnp.dot(own_feat[2], ws[512:768, cols], preferred_element_type=F32)
        preact = own.astype(BF).astype(F32) + aggregate * inverse + bias[:, cols]
        small = jnp.exp(jnp.minimum(preact, 0.0))
        above = preact > 0
        out_ref[:, cols] = jnp.where(above, preact, small - 1.0).astype(BF)
        grad = cotangent[:, cols].astype(F32) * jnp.where(above, 1.0, small)
        grounded[:, cols] = grad.astype(BF)
        scaled[:, cols] = (grad * inverse).astype(BF)
        bsum[:, cols] = jnp.sum(grad, axis=0, keepdims=True)
        return carry

    lax.fori_loop(0, 4, layer_step, 0)

    lanes = pl.ds(pl.multiple_of(c * 128, 128), 128)
    turned = (((1,), (1,)), ((), ()))

    def spread_ref(n, s, d):
        who = ((y + 4 - d) % 4) * 2 + (xh + s) % 2
        return sgt.at[pl.ds(n * 256, 256), pl.ds(pl.multiple_of(who * 128, 128), 128)]

    def spread_side(n):
        ref = spread_ref(n, 0, 0)
        return remote(ref, ref, sx_s.at[n], sx_r.at[n], far_side)

    def spread_send(n, s, d):
        m = (n * 2 + s) * 4 + d
        ref = spread_ref(n, s, 0)
        return remote(ref, ref, sy_s.at[m], sy_r.at[m], y_peer(d))

    def spread_recv(n, s, d):
        m = (n * 2 + s) * 4 + d
        ref = spread_ref(n, s, d)
        return remote(ref, ref, sy_s.at[m], sy_r.at[m], y_peer(d))

    def spread_more(n, sides):
        for s in sides:
            if s == 1:
                spread_side(n).wait_recv()
            for d in range(1, 4):
                spread_send(n, s, d).start()

    for n in range(3):
        part_rows = pl.ds(n * 256, 256)
        sgt[part_rows, lanes] = lax.dot_general(
            wn[part_rows, :], scaled[...], turned, preferred_element_type=F32
        ).astype(BF)
        spread_side(n).start()
        if n == 0:
            spread_more(0, (0,))
    for n in range(3):
        part_rows = pl.ds(n * 256, 256)
        value = lax.dot_general(
            ws[part_rows, :], grounded[...], turned, preferred_element_type=F32
        ).astype(BF)
        for d in range(4):
            tblock[d, n] = value[d * 64 : (d + 1) * 64]

    def self_send(d):
        return remote(tblock.at[d], trecv.at[d], t_s.at[d], t_r.at[d], holder(d))

    for d in range(4):

        @pl.when(jnp.logical_not(is_here(holder(d))))
        def _():
            self_send(d).start()

        @pl.when(is_here(holder(d)))
        def _():
            trecv[d] = tblock[d]

    def self_wait():
        for d in range(4):

            @pl.when(jnp.logical_not(is_here(target(d))))
            def _():
                self_send(d).wait_recv()

    flipped = (((0,), (0,)), ((), ()))

    def part(j):
        return pl.ds(j * 256, 256)

    def other_send(j):
        return remote(other.at[part(j)], other_recv.at[part(j)], ot_s.at[j], ot_r.at[j], partner)

    def ar_other():
        @pl.when(core == 0)
        def _():
            for n in range(3):
                x_mine[:, n * 256 : (n + 1) * 256] = own_feat[n]
            y_mine[...] = grounded[...]
            y_other[...] = scaled[...]

        @pl.when(core == 1)
        def _():
            x_mine[...] = x_other[...]
            for n in range(3):
                x_other[:, n * 256 : (n + 1) * 256] = own_feat[n]
            y_mine[...] = scaled[...]
            y_other[...] = grounded[...]

        for j in range(3):
            other[part(j), :] = lax.dot_general(
                x_other[:, part(j)], y_other[...], flipped, preferred_element_type=F32
            ).astype(BF)
            other_send(j).start()

    def stage1(j, d):
        axis = axis_orders[j][0]
        rows = pl.ds(pl.multiple_of(j * 256 + ((here[axis] + d) % 4) * 64, 64), 64)
        n = j * 3 + d - 1
        return remote(partial.at[rows], r1.at[n], a1_s.at[n], a1_r.at[n], along(axis, d))

    bias_slots = (bx, by, bz)

    def bias_send(axis, d):
        n = axis * 3 + d - 1
        slot = bias_slots[axis].at[here[axis]]
        return remote(slot, slot, b_s.at[n], b_r.at[n], along(axis, d))

    def bias_recv(axis, d):
        n = axis * 3 + d - 1
        slot = bias_slots[axis].at[(here[axis] + 4 - d) % 4]
        return remote(slot, slot, b_s.at[n], b_r.at[n], along(axis, d))

    def bias_start(axis, value):
        bias_slots[axis][here[axis]] = value
        for d in range(1, 4):
            bias_send(axis, d).start()

    def bias_total(axis):
        for d in range(1, 4):
            bias_recv(axis, d).wait_recv()
        slots = bias_slots[axis]
        return (slots[0] + slots[1]) + (slots[2] + slots[3])

    def ar_mine():
        for j in range(3):
            mine_part = lax.dot_general(
                x_mine[:, part(j)], y_mine[...], flipped, preferred_element_type=F32
            )
            other_send(j).wait_recv()
            partial[part(j), :] = (mine_part + other_recv[part(j), :].astype(F32)).astype(BF)
            for d in range(1, 4):
                stage1(j, d).start()

        bias_start(0, jnp.concatenate([bsum[:, i * 128 : (i + 1) * 128] for i in range(8)], axis=0))

    def pair_send(n, d):
        m = n * 4 + d
        return remote(halves.at[n, d, 1 - core], pair_recv.at[n, d], pd_s.at[m], pd_r.at[m], partner)

    def row_out(n, d):
        m = n * 4 + d
        return remote(row_send.at[n, d], row_recv.at[n, d - 1], rz_s.at[m], rz_r.at[m], z_peer(d))

    def row_side(n):
        return remote(side_send.at[n], side_recv.at[n], rl_s.at[n], rl_r.at[n], x_side)

    def pair_sum(n, d):
        pair_send(n, d).wait_recv()
        row_group[n] = halves[n, d, core].astype(F32) + pair_recv[n, d].astype(F32)
        q = (4 - d) % 4
        rows = pl.ds(pl.multiple_of(q * 64, 64), 64)
        row_group[n, xl, rows, :] = row_group[n, xl, rows, :] + trecv[q, n].astype(F32)
        return row_group[n]

    def back(n):
        for s in range(2):
            for d in range(1, 4):
                spread_recv(n, s, d).wait_recv()

        def back_step(t, carry):
            d = (t + 1) % 4
            for side in range(2):
                chip = side * 4 + (z + d) % 4
                where = pl.ds(pl.multiple_of(chip * 256, 256), 256)
                value = jnp.dot(
                    sgt[n * 256 : (n + 1) * 256, :], tile[:, where], preferred_element_type=F32
                )
                halves[n, d, 0, side] = value[:, :128].astype(BF)
                halves[n, d, 1, side] = value[:, 128:].astype(BF)
            pair_send(n, d).start()

            @pl.when(t > 0)
            def _():
                row_send[n, t] = pair_sum(n, t).astype(BF)
                row_out(n, t).start()

            return carry

        lax.fori_loop(0, 4, back_step, 0)
        pair_sum(n, 0)

    def row_cross(n):
        for d in range(1, 4):
            row_out(n, d).wait_recv()
        total = row_group[n]
        for d in range(3):
            total = total + row_recv[n, d].astype(F32)
        row_group[n] = total
        side_send[n] = row_group[n, 1 - xl].astype(BF)
        row_side(n).start()

    def row_finish(n):
        rows = slice(n * 256, (n + 1) * 256)
        row_side(n).wait_recv()
        total = row_group[n, xl] + side_recv[n].astype(F32)
        gin_ref[:, rows] = total.T.astype(BF)

    def stage2(j, d):
        axis = axis_orders[j][1]
        rows = pl.ds(pl.multiple_of(((here[axis] + d) % 4) * 16, 16), 16)
        n = j * 3 + d - 1
        return remote(q1.at[j, rows], r2.at[n], a2_s.at[n], a2_r.at[n], along(axis, d))

    def stage3(j, d):
        axis = axis_orders[j][2]
        cols = pl.ds(pl.multiple_of(((here[axis] + d) % 4) * 256, 256), 256)
        n = j * 3 + d - 1
        return remote(q2.at[j, :, cols], r3.at[n], a3_s.at[n], a3_r.at[n], along(axis, d))

    def ar_sum1():
        for j in range(3):
            axis = axis_orders[j][0]
            for d in range(1, 4):
                stage1(j, d).wait_recv()
            rows = pl.ds(pl.multiple_of(j * 256 + here[axis] * 64, 64), 64)
            total = partial[rows, :].astype(F32)
            for d in range(3):
                total = total + r1[j * 3 + d].astype(F32)
            q1[j] = total
            for d in range(1, 4):
                stage2(j, d).start()
        bias_start(1, bias_total(0))

    def ar_sum2():
        for j in range(3):
            axis = axis_orders[j][1]
            for d in range(1, 4):
                stage2(j, d).wait_recv()
            total = q1[j, pl.ds(pl.multiple_of(here[axis] * 16, 16), 16), :]
            for d in range(3):
                total = total + r2[j * 3 + d]
            q2[j] = total
            for d in range(1, 4):
                stage3(j, d).start()
        bias_start(2, bias_total(1))

    def place(j, shift, axis_step):
        a, b, e = axis_orders[j]
        spot = list(here)
        moving = axis_orders[j][axis_step]
        spot[moving] = (spot[moving] + 4 - shift) % 4
        start = j * 256 + spot[a] * 64
        if axis_step == 0:
            return result.at[pl.ds(pl.multiple_of(start, 64), 64)]
        rows = pl.ds(pl.multiple_of(start + spot[b] * 16, 16), 16)
        if axis_step == 1:
            return result.at[rows]
        return result.at[rows, pl.ds(pl.multiple_of(spot[e] * 256, 256), 256)]

    def back_copy(j, d, axis_step, shift, sends, recvs):
        n = j * 3 + d - 1
        ref = place(j, shift, axis_step)
        return remote(ref, ref, sends.at[n], recvs.at[n], along(axis_orders[j][axis_step], d))

    def bias_pair(slot):
        return remote(bk.at[slot], bk.at[slot], b_s.at[9], b_r.at[9], partner)

    def ar_sum3():
        for j in range(3):
            axis = axis_orders[j][2]
            for d in range(1, 4):
                stage3(j, d).wait_recv()
            cols = pl.ds(pl.multiple_of(here[axis] * 256, 256), 256)
            total = q2[j, :, cols]
            for d in range(3):
                total = total + r3[j * 3 + d]
            place(j, 0, 2)[...] = total.astype(BF)
            for d in range(1, 4):
                back_copy(j, d, 2, 0, g3_s, g3_r).start()
        bias_core = bias_total(2)
        bk[core] = bias_core

        bias_pair(core).start()

    def ar_gather2():
        for j in range(3):
            for d in range(1, 4):
                back_copy(j, d, 2, d, g3_s, g3_r).wait_recv()
            for d in range(1, 4):
                back_copy(j, d, 1, 0, g2_s, g2_r).start()

    def ar_gather1():
        for j in range(3):
            for d in range(1, 4):
                back_copy(j, d, 1, d, g2_s, g2_r).wait_recv()
            for d in range(1, 4):
                back_copy(j, d, 0, 0, g1_s, g1_r).start()

    def finish_rows(j, d):
        spot = (here[axis_orders[j][0]] + 4 - d) % 4
        return pl.ds(pl.multiple_of(j * 256 + spot * 64, 64), 64)

    def finish_copy(j, d):
        n = j * 4 + d
        rows = finish_rows(j, d)
        return remote(result.at[rows], result2.at[rows], fin_s.at[n], fin_r.at[n], partner)

    def own_out(j, d):
        ref = result.at[finish_rows(j, d)]
        return pltpu.make_async_copy(ref, g_ref.at[core, finish_rows(j, d)], w1_sem.at[j * 4 + d])

    def pair_out(j, d):
        ref = result2.at[finish_rows(j, d)]
        return pltpu.make_async_copy(
            ref, g_ref.at[1 - core, finish_rows(j, d)], w2_sem.at[j * 4 + d]
        )

    def ar_hand():
        for j in range(3):
            finish_copy(j, 0).start()
            own_out(j, 0).start()

    def ar_finish():
        for j in range(3):
            for d in range(1, 4):
                back_copy(j, d, 0, d, g1_s, g1_r).wait_recv()
                finish_copy(j, d).start()
                own_out(j, d).start()
        bias_pair(1 - core).wait_recv()
        total = bk[0] + bk[1]
        gbias_ref[...] = jnp.concatenate([total[i : i + 1, :] for i in range(8)], axis=1)
        for j in range(3):
            for d in range(4):
                finish_copy(j, d).wait_recv()
                pair_out(j, d).start()

    spread_more(0, (1,))
    spread_more(1, (0, 1))
    ar_other()
    spread_more(2, (0, 1))
    ar_mine()
    self_wait()
    back(0)
    back(1)
    ar_sum1()
    back(2)
    row_cross(0)
    ar_sum2()
    row_cross(1)
    ar_sum3()
    row_cross(2)
    ar_gather2()
    ar_gather1()
    ar_hand()

    for n in range(3):
        row_finish(n)
    ar_finish()

    for d in range(4):

        @pl.when(jnp.logical_not(is_here(target(d))))
        def _():
            for n in range(3):
                permute(n, d).wait_send()

        @pl.when(jnp.logical_not(is_here(holder(d))))
        def _():
            self_send(d).wait_send()

    def drain_forward():
        for n in range(3):
            side_gather(n).wait_send()
            cross(n).wait_send()
            for d in range(1, 4):
                reduce_send(n, d).wait_send()
            for s in range(2):
                for d in range(1, 4):
                    gather_send(n, s, d).wait_send()
                for d in range(4):
                    forward(n, s, d).wait_send()
        for d in range(1, 4):
            mass_send(d).wait_send()
        mass_side().wait_send()

    def drain_back():
        for n in range(3):
            spread_side(n).wait_send()
            row_side(n).wait_send()
            for d in range(4):
                pair_send(n, d).wait_send()
            for d in range(1, 4):
                row_out(n, d).wait_send()
                for s in range(2):
                    spread_send(n, s, d).wait_send()

    def drain_ar():
        for j in range(3):
            other_send(j).wait_send()
            for d in range(1, 4):
                stage1(j, d).wait_send()
                stage2(j, d).wait_send()
                stage3(j, d).wait_send()
                back_copy(j, d, 2, 0, g3_s, g3_r).wait_send()
                back_copy(j, d, 1, 0, g2_s, g2_r).wait_send()
                back_copy(j, d, 0, 0, g1_s, g1_r).wait_send()
                bias_send(j, d).wait_send()
            for d in range(4):
                finish_copy(j, d).wait_send()
                own_out(j, d).wait()
                pair_out(j, d).wait()
        bias_pair(core).wait_send()

    drain_forward()
    drain_back()
    drain_ar()


def layer(tile, mass, features, w_neigh, w_self, bias, cotangent):
    vmem = pl.BlockSpec(memory_space=pltpu.VMEM)
    hbm = pl.BlockSpec(memory_space=pl.ANY)
    sem = pltpu.SemaphoreType.DMA
    V = pltpu.VMEM
    shape = jax.ShapeDtypeStruct
    return pl.pallas_call(
        layer_kernel,
        out_shape=(
            shape((128, 1024), BF),
            shape((128, 768), BF),
            shape((2, 768, 1024), BF),
            shape((1, 1024), F32),
        ),
        in_specs=[hbm, vmem, vmem, hbm, hbm, vmem, vmem],
        out_specs=(vmem, vmem, hbm, vmem),
        scratch_shapes=[
            V((1024, 2048), BF), V((768, 1024), BF), V((768, 1024), BF), sem((3,)),
            V((3, 2048, 256), BF), V((3, 128, 256), BF), V((3, 4, 256, 256), BF),
            V((3, 3, 256, 256), BF), V((3, 128, 256), BF), V((3, 128, 256), BF),
            V((3, 2, 8, 128), F32), V((8, 128), F32), V((2, 8, 128), F32), V((128, 768), F32),
            V((3, 2, 128, 256), F32),
            V((128, 1024), BF), V((128, 1024), BF), V((768, 1024), BF), V((4, 3, 64, 128), BF), V((4, 3, 64, 128), BF),
            V((128, 768), BF), V((128, 1024), BF), V((128, 768), BF), V((128, 1024), BF),
            V((768, 1024), BF), V((768, 1024), BF), V((768, 1024), BF),
            V((9, 64, 1024), BF), V((3, 64, 1024), F32), V((9, 16, 1024), F32), V((3, 16, 1024), F32),
            V((9, 16, 256), F32), V((768, 1024), BF), V((768, 1024), BF),
            V((3, 4, 2, 2, 256, 128), BF), V((3, 4, 2, 256, 128), BF), V((3, 4, 2, 256, 128), BF),
            V((3, 3, 2, 256, 128), BF), V((3, 2, 256, 128), F32), V((3, 256, 128), BF), V((3, 256, 128), BF),
            V((1, 1024), F32), V((4, 8, 128), F32), V((4, 8, 128), F32), V((4, 8, 128), F32), V((2, 8, 128), F32),
        ]
        + [sem((3,))] * 2 + [sem((24,))] * 4 + [sem((12,))] * 2 + [sem((4,))] * 2 + [sem((12,))] * 2
        + [sem((3,))] * 4 + [sem((24,))] * 2 + [sem((4,))] * 2 + [sem((3,))] * 2
        + [sem((9,))] * 12 + [sem((12,))] * 2 + [sem((10,))] * 2 + [sem((12,))] * 4 + [sem((3,))] * 2
        + [sem((12,))] * 2,
        compiler_params=pltpu.CompilerParams(
            collective_id=0, has_side_effects=True, vmem_limit_bytes=58 * 1024 * 1024
        ),
        name="layer",
    )(tile, mass, features, w_neigh, w_self, bias, cotangent)


def local(
    features, w_neigh, w_self, bias, cotangent, block_rows, block_cols, block_vals, block_count
):
    row_size = lax.axis_size("row")
    col_size = lax.axis_size("col")
    node_dev = features.shape[0]
    tile, mass = densify(
        block_vals[0, 0], block_rows[0, 0], block_cols[0, 0], block_count[0], col_size, row_size
    )
    output, grad_input, grads, g_bias = layer(
        tile, mass, features, w_neigh, w_self, bias.reshape(1, -1), cotangent
    )
    factor = 1.0 / math.sqrt(node_dev * row_size * col_size)
    grad_self, grad_neigh, output, grad_input, g_bias = finish(
        grads, output, grad_input, g_bias, factor, 32.0 * factor
    )
    return output, grad_input, grad_self, grad_neigh, g_bias.reshape(-1)


def solution(mesh):
    in_specs = (
        P(("col", "row"), None),
        P(),
        P(),
        P(),
        P(("row", "col"), None),
        P("row", "col", None),
        P("row", "col", None),
        P("row", "col", None, None, None),
        P("row", "col"),
    )
    out_specs = (P(("row", "col"), None), P(("col", "row"), None), P(), P(), P())
    return jax.shard_map(local, mesh=mesh, in_specs=in_specs, out_specs=out_specs, check_vma=False)
```

```python
import functools
import math

import jax
import jax.numpy as jnp
from jax import lax
from jax.experimental import pallas as pl
from jax.experimental.pallas import tpu as pltpu
from jax.sharding import PartitionSpec as P


def densify_kernel(
    rows_hbm, cols_hbm, count_hbm, vals_hbm, tile, mass_ref,
    rows_ref, cols_ref, count_ref, vals, acc, in_sem, id_sem,
):
    row_blocks, col_blocks, size, _ = acc.shape
    pieces = 4
    span = vals.shape[0] // pieces

    def load(q):
        slots = pl.ds(q * span, span)
        return pltpu.make_async_copy(vals_hbm.at[slots], vals.at[slots], in_sem.at[q])

    ids = [
        pltpu.make_async_copy(rows_hbm, rows_ref, id_sem.at[0]),
        pltpu.make_async_copy(cols_hbm, cols_ref, id_sem.at[1]),
        pltpu.make_async_copy(count_hbm, count_ref, id_sem.at[2]),
    ]
    for copy in ids:
        copy.start()
    for q in range(pieces):
        load(q).start()

    def clear(i, carry):
        for j in range(col_blocks):
            acc[i, j] = jnp.zeros((size, size), jnp.float32)
        return carry

    lax.fori_loop(0, row_blocks, clear, 0)

    def add(s, carry):
        i = rows_ref[s]
        j = cols_ref[s]
        acc[i, j] += vals[s].astype(jnp.float32)
        return carry

    for copy in ids:
        copy.wait()
    count = count_ref[0]
    for q in range(pieces):
        load(q).wait()
        lax.fori_loop(q * span, jnp.minimum(count, (q + 1) * span), add, 0)
    diagonal = lax.broadcasted_iota(jnp.int32, (size, size), 0) == lax.broadcasted_iota(
        jnp.int32, (size, size), 1
    )

    def finish(i, carry):
        total = jnp.zeros((size, size), jnp.float32)
        start = pl.multiple_of(i * size, size)
        for j in range(col_blocks):
            block = acc[i, j]
            total = total + block
            tile[pl.ds(start, size), j * size : (j + 1) * size] = block.astype(jnp.bfloat16)
        sums = jnp.sum(total, axis=1, keepdims=True)
        as_row = jnp.sum(jnp.where(diagonal, sums, 0.0), axis=0, keepdims=True)
        mass_ref[i] = jnp.broadcast_to(as_row, (8, size))
        return carry

    lax.fori_loop(0, row_blocks, finish, 0)


def densify(values, row_ids, col_ids, live_count, row_blocks, col_blocks):
    slots, size, _ = values.shape
    hbm = pl.BlockSpec(memory_space=pltpu.HBM)
    vmem = pl.BlockSpec(memory_space=pltpu.VMEM)
    rows, cols = row_blocks * size, col_blocks * size
    return pl.pallas_call(
        densify_kernel,
        out_shape=(
            jax.ShapeDtypeStruct((rows, cols), jnp.bfloat16),
            jax.ShapeDtypeStruct((row_blocks, 8, size), jnp.float32),
        ),
        in_specs=[hbm, hbm, hbm, hbm],
        out_specs=(vmem, vmem),
        scratch_shapes=[
            pltpu.SMEM((slots,), jnp.int32),
            pltpu.SMEM((slots,), jnp.int32),
            pltpu.SMEM((1,), jnp.int32),
            pltpu.VMEM((slots, size, size), jnp.bfloat16),
            pltpu.VMEM((row_blocks, col_blocks, size, size), jnp.float32),
            pltpu.SemaphoreType.DMA((4,)),
            pltpu.SemaphoreType.DMA((3,)),
        ],
        compiler_params=pltpu.CompilerParams(vmem_limit_bytes=18 * 1024 * 1024),
        name="densify",
    )(row_ids, col_ids, live_count, values)


def finish_kernel(
    own_scale, neigh_scale, grads, out_in, gin_in, bias_in,
    own_to, neigh_to, out_to, gin_to, bias_to, wide, out_sem,
):
    pieces = out_sem.shape[0]
    rows = grads.shape[1]
    step = 2 * rows // pieces
    stores = []
    for p in range(pieces):
        which, at = p % 2, pl.ds(p // 2 * step, step)
        target = (own_to, neigh_to)[which]
        scale = (own_scale, neigh_scale)[which]
        wide[which, at] = grads[which, at].astype(jnp.float32) * scale
        stores.append(pltpu.make_async_copy(wide.at[which, at], target.at[at], out_sem.at[p]))
        stores[p].start()
    bias_to[...] = bias_in[...] * own_scale
    out_to[...] = out_in[...]
    gin_to[...] = gin_in[...]
    for copy in stores:
        copy.wait()


def finish(grads, output, grad_input, g_bias, own_scale, neigh_scale):
    _, rows, cols = grads.shape
    hbm = pl.BlockSpec(memory_space=pltpu.HBM)
    vmem = pl.BlockSpec(memory_space=pltpu.VMEM)
    shape = jax.ShapeDtypeStruct
    wide = shape((rows, cols), jnp.float32)
    pieces = 12
    return pl.pallas_call(
        functools.partial(finish_kernel, own_scale, neigh_scale),
        out_shape=(
            wide,
            wide,
            shape(output.shape, output.dtype),
            shape(grad_input.shape, grad_input.dtype),
            shape(g_bias.shape, g_bias.dtype),
        ),
        in_specs=[vmem, vmem, vmem, vmem],
        out_specs=(hbm, hbm, vmem, vmem, vmem),
        scratch_shapes=[
            pltpu.VMEM((2, rows, cols), jnp.float32),
            pltpu.SemaphoreType.DMA((pieces,)),
        ],
        compiler_params=pltpu.CompilerParams(vmem_limit_bytes=24 * 1024 * 1024),
        name="finish",
    )(grads, output, grad_input, g_bias)


MESH = pl.DeviceIdType.MESH
LAYER_VMEM = 36
BF = jnp.bfloat16
F32 = jnp.float32


def remote(src, dst, send, recv, device):
    return pltpu.make_async_remote_copy(
        src_ref=src, dst_ref=dst, send_sem=send, recv_sem=recv, device_id=device, device_id_type=MESH
    )


def layer_kernel(
    tile, mass, features, wn_hbm, ws_hbm, bias, cotangent,
    out_ref, gin_ref, g_ref, gbias_ref,
    wn, ws, local_sem,
    fg, own_feat, send_blocks, recv_blocks, cross_send, cross_recv,
    mass_recv, mass_cross, mass_sum, mixed, group,
    scaled, grounded, sgt, tblock, trecv,
    x_mine, y_mine, x_other, y_other, other, other_recv, partial,
    r1, q1, r2, q2, r3, result, result2,
    halves, pair_recv, row_send, row_recv, row_group, side_send, side_recv,
    bsum, bx, by, bz, bk,
    gx_s, gx_r, gz_s, gz_r, fw_s, fw_r, pm_s, pm_r, ms_s, ms_r, rs_s, rs_r, rx_s, rx_r,
    sx_s, sx_r, sy_s, sy_r, t_s, t_r,
    ot_s, ot_r, a1_s, a1_r, a2_s, a2_r, a3_s, a3_r, g3_s, g3_r, g2_s, g2_r, g1_s, g1_r, fin_s, fin_r,
    b_s, b_r, pd_s, pd_r, rz_s, rz_r, rl_s, rl_r,
):
    r = lax.axis_index("row")
    c = lax.axis_index("col")
    xl, z, core = r // 8, (r // 2) % 4, r % 2
    y, xh = c // 2, c % 2
    x = xh * 2 + xl

    def device_of(px, py, pz):
        return (((px % 2) * 4 + pz) * 2 + core, py * 2 + px // 2)

    here = (x, y, z)
    axis_orders = ((0, 1, 2), (2, 0, 1), (0, 1, 2))
    gather_orders = ((2, 1, 0), (1, 0, 2), (2, 0, 1))

    def along(axis, d):
        spot = list(here)
        spot[axis] = (spot[axis] + d) % 4
        return device_of(*spot)

    partner = (r + 1 - 2 * core, c)
    here_id = r * 8 + c
    block = r * 8 + c
    first, first_col = block % 16, block // 16

    def target(d):
        from_row = (xl * 4 + (z + 4 - d) % 4) * 2 + core
        node = c * 16 + from_row
        return node // 8, node % 8

    def holder(d):
        chip = first // 8 * 4 + (first // 2 + d) % 4
        return chip * 2 + first % 2, first_col

    def is_here(device):
        return device[0] * 8 + device[1] == here_id

    copies = [
        pltpu.make_async_copy(ws_hbm, ws, local_sem.at[1]),
        pltpu.make_async_copy(wn_hbm, wn, local_sem.at[2]),
    ]
    for copy in copies:
        copy.start()

    barrier = pltpu.get_barrier_semaphore()

    def hello(device):
        pl.semaphore_signal(barrier, inc=1, device_id=device, device_id_type=MESH)

    x_side = (((1 - xl) * 4 + z) * 2 + core, c)
    far_side = (r, y * 2 + 1 - xh)

    def z_peer(d):
        return ((xl * 4 + (z + d) % 4) * 2 + core, c)

    def y_peer(d):
        return (r, ((y + d) % 4) * 2 + xh)

    for d in range(1, 4):
        hello(z_peer(d))
        hello(y_peer(d))
    hello(x_side)
    hello(far_side)
    hello(partner)
    hello((((1 - xl) * 4 + z) * 2 + core, y * 2 + 1 - xh))

    remote_peers = 10
    for d in range(4):
        for device in (target(d), holder(d)):
            away = jnp.logical_not(is_here(device))
            remote_peers = remote_peers + away.astype(jnp.int32)

            @pl.when(away)
            def _():
                hello(device)

    pl.semaphore_wait(barrier, remote_peers)

    for n in range(3):
        fg[n, pl.ds(r * 128, 128), :] = features[:, n * 256 : (n + 1) * 256]

    def source_rows_start(s, d, k):
        chip = ((xl + s) % 2) * 4 + (z + 4 - d) % 4
        return (chip * 2 + k) * 128

    def source_rows(s, d, k):
        return pl.ds(pl.multiple_of(source_rows_start(s, d, k), 128), 128)

    def side_gather(n):
        ref = fg.at[n, source_rows(0, 0, core)]
        return remote(ref, ref, gx_s.at[n], gx_r.at[n], x_side)

    def gather_send(n, s, d):
        m = (n * 2 + s) * 4 + d
        ref = fg.at[n, source_rows(s, 0, core)]
        return remote(ref, ref, gz_s.at[m], gz_r.at[m], z_peer(d))

    def gather_recv(n, s, d):
        m = (n * 2 + s) * 4 + d
        ref = fg.at[n, source_rows(s, d, core)]
        return remote(ref, ref, gz_s.at[m], gz_r.at[m], z_peer(d))

    def forward(n, s, d):
        m = (n * 2 + s) * 4 + d
        ref = fg.at[n, source_rows(s, d, core)]
        return remote(ref, ref, fw_s.at[m], fw_r.at[m], partner)

    def own_piece(n, d):
        return own_feat.at[n, pl.ds(d * 32, 32)]

    def permute(n, d):
        start = source_rows_start(0, d, core) + d * 32
        rows = pl.ds(pl.multiple_of(start, 32), 32)
        m = d * 3 + n
        return remote(fg.at[n, rows], own_piece(n, d), pm_s.at[m], pm_r.at[m], target(d))

    def permute_start(n):
        for d in range(4):

            @pl.when(jnp.logical_not(is_here(target(d))))
            def _():
                permute(n, d).start()

            @pl.when(is_here(target(d)))
            def _():
                start = source_rows_start(0, d, core) + d * 32
                own_feat[n, d * 32 : (d + 1) * 32, :] = fg[n, pl.ds(pl.multiple_of(start, 32), 32), :]

    def permute_wait(n):
        for d in range(4):

            @pl.when(jnp.logical_not(is_here(holder(d))))
            def _():
                permute(n, d).wait_recv()

    def mass_send(d):
        to = ((y + d) % 4) * 2
        return remote(mass.at[pl.ds(to, 2)], mass_recv.at[d - 1], ms_s.at[d], ms_r.at[d], y_peer(d))

    def mass_side():
        return remote(mass_sum.at[1 - xh], mass_cross, ms_s.at[0], ms_r.at[0], far_side)

    def spread_gather(n):
        side_gather(n).wait_recv()
        for s in range(2):
            for d in range(1, 4):
                gather_send(n, s, d).start()

    for n in range(3):
        side_gather(n).start()
    for d in range(1, 4):
        gather_send(0, 0, d).start()
    for d in range(1, 4):
        mass_send(d).start()
    side_gather(0).wait_recv()
    for d in range(1, 4):
        gather_send(0, 1, d).start()
    spread_gather(1)


    def reduce_send(n, d):
        m = n * 4 + d
        return remote(
            send_blocks.at[n, d], recv_blocks.at[n, d - 1], rs_s.at[m], rs_r.at[m], y_peer(d)
        )

    def cross(n):
        return remote(cross_send.at[n], cross_recv.at[n], rx_s.at[n], rx_r.at[n], far_side)

    def mix(n):
        for s in range(2):
            forward(n, s, 0).start()
        for s in range(2):
            for d in range(1, 4):
                gather_recv(n, s, d).wait_recv()
                forward(n, s, d).start()
        if n == 0:
            spread_gather(2)
        for s in range(2):
            for d in range(4):
                forward(n, s, d).wait_recv()

        def mix_step(t, carry):
            d = (t + 1) % 4
            rows = pl.ds(pl.multiple_of(((y + d) % 4) * 256, 256), 256)
            value = jnp.dot(tile[rows, :], fg[n], preferred_element_type=F32)

            @pl.when(t < 3)
            def _():
                send_blocks[n, d] = value.astype(BF)
                reduce_send(n, d).start()

            @pl.when(t == 3)
            def _():
                group[n, 0] = value[:128]
                group[n, 1] = value[128:]

            return carry

        lax.fori_loop(0, 4, mix_step, 0)

    def cross_start(n):
        for d in range(1, 4):
            reduce_send(n, d).wait_recv()
        for h in range(2):
            total = group[n, h]
            for d in range(3):
                total = total + recv_blocks[n, d, h * 128 : (h + 1) * 128].astype(F32)
            group[n, h] = total
        cross_send[n] = group[n, 1 - xh].astype(BF)
        cross(n).start()

    mix(0)
    permute_start(0)
    mix(1)
    permute_start(1)
    cross_start(0)
    for d in range(1, 4):
        mass_send(d).wait_recv()
    for h in range(2):
        mass_sum[h] = mass[y * 2 + h] + ((mass_recv[0, h] + mass_recv[1, h]) + mass_recv[2, h])
    mass_side().start()
    mix(2)
    permute_start(2)
    cross_start(1)
    cross_start(2)
    for copy in copies:
        copy.wait()

    for n in range(3):
        permute_wait(n)
    mass_side().wait_recv()
    degree = mass_sum[xh] + mass_cross[...]
    for n in range(3):
        cross(n).wait_recv()
        mixed[:, n * 256 : (n + 1) * 256] = group[n, xh] + cross_recv[n].astype(F32)

    diagonal = lax.broadcasted_iota(jnp.int32, (128, 128), 0) == lax.broadcasted_iota(
        jnp.int32, (128, 128), 1
    )
    column = jnp.sum(jnp.where(diagonal, degree[0:1, :], 0.0), axis=1, keepdims=True)
    inverse = 1.0 / (column + 1.0)
    high = mixed[...].astype(BF)
    low = (mixed[...] - high.astype(F32)).astype(BF)
    mixed_high = x_other
    mixed_high[...] = high
    x_mine[...] = low

    def layer_step(n, carry):
        cols = pl.ds(pl.multiple_of(n * 256, 256), 256)
        aggregate = jnp.dot(mixed_high[...], wn[:, cols], preferred_element_type=F32)
        aggregate += jnp.dot(x_mine[...], wn[:, cols], preferred_element_type=F32)
        own = jnp.dot(own_feat[0], ws[0:256, cols], preferred_element_type=F32)
        own += jnp.dot(own_feat[1], ws[256:512, cols], preferred_element_type=F32)
        own += jnp.dot(own_feat[2], ws[512:768, cols], preferred_element_type=F32)
        preact = own.astype(BF).astype(F32) + aggregate * inverse + bias[:, cols]
        small = jnp.exp(jnp.minimum(preact, 0.0))
        above = preact > 0
        out_ref[:, cols] = jnp.where(above, preact, small - 1.0).astype(BF)
        grad = cotangent[:, cols].astype(F32) * jnp.where(above, 1.0, small)
        grounded[:, cols] = grad.astype(BF)
        scaled[:, cols] = (grad * inverse).astype(BF)
        bsum[:, cols] = jnp.sum(grad, axis=0, keepdims=True)
        return carry

    lax.fori_loop(0, 4, layer_step, 0)

    lanes = pl.ds(pl.multiple_of(c * 128, 128), 128)
    turned = (((1,), (1,)), ((), ()))

    def spread_ref(n, s, d):
        who = ((y + 4 - d) % 4) * 2 + (xh + s) % 2
        return sgt.at[pl.ds(n * 256, 256), pl.ds(pl.multiple_of(who * 128, 128), 128)]

    def spread_side(n):
        ref = spread_ref(n, 0, 0)
        return remote(ref, ref, sx_s.at[n], sx_r.at[n], far_side)

    def spread_send(n, s, d):
        m = (n * 2 + s) * 4 + d
        ref = spread_ref(n, s, 0)
        return remote(ref, ref, sy_s.at[m], sy_r.at[m], y_peer(d))

    def spread_recv(n, s, d):
        m = (n * 2 + s) * 4 + d
        ref = spread_ref(n, s, d)
        return remote(ref, ref, sy_s.at[m], sy_r.at[m], y_peer(d))

    def spread_more(n, sides):
        for s in sides:
            if s == 1:
                spread_side(n).wait_recv()
            for d in range(1, 4):
                spread_send(n, s, d).start()

    for n in range(3):
        part_rows = pl.ds(n * 256, 256)
        sgt[part_rows, lanes] = lax.dot_general(
            wn[part_rows, :], scaled[...], turned, preferred_element_type=F32
        ).astype(BF)
        spread_side(n).start()
        if n == 0:
            spread_more(0, (0,))
    def self_send(d):
        return remote(tblock.at[d], trecv.at[d], t_s.at[d], t_r.at[d], holder(d))

    def self_wait():
        for d in range(4):

            @pl.when(jnp.logical_not(is_here(target(d))))
            def _():
                self_send(d).wait_recv()

    flipped = (((0,), (0,)), ((), ()))

    def part(j):
        return pl.ds(j * 256, 256)

    def other_send(j):
        return remote(other.at[part(j)], other_recv.at[part(j)], ot_s.at[j], ot_r.at[j], partner)

    def ar_other():
        @pl.when(core == 0)
        def _():
            for n in range(3):
                x_mine[:, n * 256 : (n + 1) * 256] = own_feat[n]
            y_mine[...] = grounded[...]
            y_other[...] = scaled[...]

        @pl.when(core == 1)
        def _():
            x_mine[...] = x_other[...]
            for n in range(3):
                x_other[:, n * 256 : (n + 1) * 256] = own_feat[n]
            y_mine[...] = scaled[...]
            y_other[...] = grounded[...]

        for j in range(3):
            other[part(j), :] = lax.dot_general(
                x_other[:, part(j)], y_other[...], flipped, preferred_element_type=F32
            ).astype(BF)
            other_send(j).start()

    def stage1(j, d):
        axis = axis_orders[j][0]
        rows = pl.ds(pl.multiple_of(j * 256 + ((here[axis] + d) % 4) * 64, 64), 64)
        n = j * 3 + d - 1
        return remote(partial.at[rows], r1.at[n], a1_s.at[n], a1_r.at[n], along(axis, d))

    bias_slots = (bx, by, bz)

    def bias_send(axis, d):
        n = axis * 3 + d - 1
        slot = bias_slots[axis].at[here[axis]]
        return remote(slot, slot, b_s.at[n], b_r.at[n], along(axis, d))

    def bias_recv(axis, d):
        n = axis * 3 + d - 1
        slot = bias_slots[axis].at[(here[axis] + 4 - d) % 4]
        return remote(slot, slot, b_s.at[n], b_r.at[n], along(axis, d))

    def bias_start(axis, value):
        bias_slots[axis][here[axis]] = value
        for d in range(1, 4):
            bias_send(axis, d).start()

    def bias_total(axis):
        for d in range(1, 4):
            bias_recv(axis, d).wait_recv()
        slots = bias_slots[axis]
        return (slots[0] + slots[1]) + (slots[2] + slots[3])

    def ar_mine():
        for j in range(3):
            mine_part = lax.dot_general(
                x_mine[:, part(j)], y_mine[...], flipped, preferred_element_type=F32
            )
            other_send(j).wait_recv()
            partial[part(j), :] = (mine_part + other_recv[part(j), :].astype(F32)).astype(BF)
            for d in range(1, 4):
                stage1(j, d).start()

        bias_start(0, jnp.concatenate([bsum[:, i * 128 : (i + 1) * 128] for i in range(8)], axis=0))

    def pair_send(n, d):
        m = n * 4 + d
        return remote(halves.at[n, d, 1 - core], pair_recv.at[n, d], pd_s.at[m], pd_r.at[m], partner)

    def row_out(n, d):
        m = n * 4 + d
        return remote(row_send.at[n, d], row_recv.at[n, d - 1], rz_s.at[m], rz_r.at[m], z_peer(d))

    def row_side(n):
        return remote(side_send.at[n], side_recv.at[n], rl_s.at[n], rl_r.at[n], x_side)

    def pair_sum(n, d):
        pair_send(n, d).wait_recv()
        row_group[n] = halves[n, d, core].astype(F32) + pair_recv[n, d].astype(F32)
        q = (4 - d) % 4
        rows = pl.ds(pl.multiple_of(q * 64, 64), 64)
        row_group[n, xl, rows, :] = row_group[n, xl, rows, :] + trecv[q, n].astype(F32)
        return row_group[n]

    def back(n):
        for s in range(2):
            for d in range(1, 4):
                spread_recv(n, s, d).wait_recv()

        def back_step(t, carry):
            d = (t + 1) % 4
            for side in range(2):
                chip = side * 4 + (z + d) % 4
                where = pl.ds(pl.multiple_of(chip * 256, 256), 256)
                value = jnp.dot(
                    sgt[n * 256 : (n + 1) * 256, :], tile[:, where], preferred_element_type=F32
                )
                halves[n, d, 0, side] = value[:, :128].astype(BF)
                halves[n, d, 1, side] = value[:, 128:].astype(BF)
            pair_send(n, d).start()
            return carry

        lax.fori_loop(0, 4, back_step, 0)

        def pair_step(d, carry):
            row_send[n, d] = pair_sum(n, d).astype(BF)
            row_out(n, d).start()
            return carry

        lax.fori_loop(1, 4, pair_step, 0)
        pair_sum(n, 0)

    def row_cross(n):
        for d in range(1, 4):
            row_out(n, d).wait_recv()
        total = row_group[n]
        for d in range(3):
            total = total + row_recv[n, d].astype(F32)
        row_group[n] = total
        side_send[n] = row_group[n, 1 - xl].astype(BF)
        row_side(n).start()

    def row_finish(n):
        rows = slice(n * 256, (n + 1) * 256)
        row_side(n).wait_recv()
        total = row_group[n, xl] + side_recv[n].astype(F32)
        gin_ref[:, rows] = total.T.astype(BF)

    def stage2(j, d):
        axis = axis_orders[j][1]
        rows = pl.ds(pl.multiple_of(((here[axis] + d) % 4) * 16, 16), 16)
        n = j * 3 + d - 1
        return remote(q1.at[j, rows], r2.at[n], a2_s.at[n], a2_r.at[n], along(axis, d))

    def stage3(j, d):
        axis = axis_orders[j][2]
        cols = pl.ds(pl.multiple_of(((here[axis] + d) % 4) * 256, 256), 256)
        n = j * 3 + d - 1
        return remote(q2.at[j, :, cols], r3.at[n], a3_s.at[n], a3_r.at[n], along(axis, d))

    def ar_sum1():
        for j in range(3):
            axis = axis_orders[j][0]
            for d in range(1, 4):
                stage1(j, d).wait_recv()
            rows = pl.ds(pl.multiple_of(j * 256 + here[axis] * 64, 64), 64)
            total = partial[rows, :].astype(F32)
            for d in range(3):
                total = total + r1[j * 3 + d].astype(F32)
            q1[j] = total
            for d in range(1, 4):
                stage2(j, d).start()
        bias_start(1, bias_total(0))

    def ar_sum2():
        for j in range(3):
            axis = axis_orders[j][1]
            for d in range(1, 4):
                stage2(j, d).wait_recv()
            total = q1[j, pl.ds(pl.multiple_of(here[axis] * 16, 16), 16), :]
            for d in range(3):
                total = total + r2[j * 3 + d]
            q2[j] = total
            for d in range(1, 4):
                stage3(j, d).start()
        bias_start(2, bias_total(1))

    def place(j, shift, step):
        a, b, e = axis_orders[j]
        order = gather_orders[j]
        spot = list(here)
        spot[order[step]] = (spot[order[step]] + 4 - shift) % 4
        lead = j * 4 + spot[a]
        if step == 0:
            return result.at[lead, spot[b], :, pl.ds(pl.multiple_of(spot[e] * 256, 256), 256)]
        if step == 1:
            return result.at[lead, spot[b]]
        return final(result, j, spot)

    def final(ref, j, spot):
        a, b, e = axis_orders[j]
        if gather_orders[j][2] == a:
            return ref.at[j * 4 + spot[a]]
        return ref.at[pl.ds(j * 4, 4), spot[b]]

    def back_copy(j, d, step, shift, sends, recvs):
        n = j * 3 + d - 1
        ref = place(j, shift, step)
        return remote(ref, ref, sends.at[n], recvs.at[n], along(gather_orders[j][step], d))

    def bias_pair(slot):
        return remote(bk.at[slot], bk.at[slot], b_s.at[9], b_r.at[9], partner)

    def ar_sum3():
        for j in range(3):
            axis = axis_orders[j][2]
            for d in range(1, 4):
                stage3(j, d).wait_recv()
            cols = pl.ds(pl.multiple_of(here[axis] * 256, 256), 256)
            total = q2[j, :, cols]
            for d in range(3):
                total = total + r3[j * 3 + d]
            place(j, 0, 0)[...] = total.astype(BF)
            for d in range(1, 4):
                back_copy(j, d, 0, 0, g3_s, g3_r).start()
        bias_core = bias_total(2)
        bk[core] = bias_core

        bias_pair(core).start()

    def ar_gather2():
        for j in range(3):
            for d in range(1, 4):
                back_copy(j, d, 0, d, g3_s, g3_r).wait_recv()
            for d in range(1, 4):
                back_copy(j, d, 1, 0, g2_s, g2_r).start()

    def ar_gather1():
        for j in range(3):
            for d in range(1, 4):
                back_copy(j, d, 1, d, g2_s, g2_r).wait_recv()
            for d in range(1, 4):
                back_copy(j, d, 2, 0, g1_s, g1_r).start()

    def last_spot(j, d):
        axis = gather_orders[j][2]
        spot = list(here)
        spot[axis] = (spot[axis] + 4 - d) % 4
        return spot

    def finish_copy(j, d):
        n = j * 4 + d
        spot = last_spot(j, d)
        return remote(
            final(result, j, spot), final(result2, j, spot), fin_s.at[n], fin_r.at[n], partner
        )

    def own_out(j, d):
        spot = last_spot(j, d)
        final(g_ref.at[core], j, spot)[...] = final(result, j, spot)[...]

    def pair_out(j, d):
        spot = last_spot(j, d)
        final(g_ref.at[1 - core], j, spot)[...] = final(result2, j, spot)[...]

    def ar_hand():
        for j in range(3):
            finish_copy(j, 0).start()
            own_out(j, 0)

    def ar_finish():
        for j in range(3):
            for d in range(1, 4):
                back_copy(j, d, 2, d, g1_s, g1_r).wait_recv()
                finish_copy(j, d).start()
                own_out(j, d)
        bias_pair(1 - core).wait_recv()
        total = bk[0] + bk[1]
        gbias_ref[...] = jnp.concatenate([total[i : i + 1, :] for i in range(8)], axis=1)
        for j in range(3):
            for d in range(4):
                finish_copy(j, d).wait_recv()
                pair_out(j, d)

    def self_start():
        for n in range(3):
            part_rows = pl.ds(n * 256, 256)
            value = lax.dot_general(
                ws[part_rows, :], grounded[...], turned, preferred_element_type=F32
            ).astype(BF)
            for d in range(4):
                tblock[d, n] = value[d * 64 : (d + 1) * 64]

        for d in range(4):

            @pl.when(jnp.logical_not(is_here(holder(d))))
            def _():
                self_send(d).start()

            @pl.when(is_here(holder(d)))
            def _():
                trecv[d] = tblock[d]

    def drain_own():
        for d in range(4):

            @pl.when(jnp.logical_not(is_here(target(d))))
            def _():
                for n in range(3):
                    permute(n, d).wait_send()

            @pl.when(jnp.logical_not(is_here(holder(d))))
            def _():
                self_send(d).wait_send()

    def drain_forward():
        for n in range(3):
            side_gather(n).wait_send()
            cross(n).wait_send()
            for d in range(1, 4):
                reduce_send(n, d).wait_send()
            for s in range(2):
                for d in range(1, 4):
                    gather_send(n, s, d).wait_send()
                for d in range(4):
                    forward(n, s, d).wait_send()
        for d in range(1, 4):
            mass_send(d).wait_send()
        mass_side().wait_send()

    def drain_back():
        for n in range(3):
            spread_side(n).wait_send()
            row_side(n).wait_send()
            for d in range(4):
                pair_send(n, d).wait_send()
            for d in range(1, 4):
                row_out(n, d).wait_send()
                for s in range(2):
                    spread_send(n, s, d).wait_send()

    def drain_ar():
        for j in range(3):
            other_send(j).wait_send()
            for d in range(1, 4):
                stage1(j, d).wait_send()
                stage2(j, d).wait_send()
                stage3(j, d).wait_send()
                back_copy(j, d, 0, 0, g3_s, g3_r).wait_send()
                back_copy(j, d, 1, 0, g2_s, g2_r).wait_send()
                bias_send(j, d).wait_send()

    def drain_last():
        for j in range(3):
            for d in range(1, 4):
                back_copy(j, d, 2, 0, g1_s, g1_r).wait_send()
            for d in range(4):
                finish_copy(j, d).wait_send()
        bias_pair(core).wait_send()

    self_start()
    spread_more(0, (1,))
    spread_more(1, (0, 1))
    ar_other()
    spread_more(2, (0, 1))
    ar_mine()
    drain_forward()
    self_wait()
    back(0)
    back(1)
    ar_sum1()
    back(2)
    row_cross(0)
    ar_sum2()
    row_cross(1)
    ar_sum3()
    row_cross(2)
    ar_gather2()
    ar_gather1()
    ar_hand()
    row_finish(0)
    row_finish(1)
    row_finish(2)
    drain_own()
    drain_back()
    drain_ar()
    ar_finish()
    drain_last()


def layer(tile, mass, features, w_neigh, w_self, bias, cotangent):
    vmem = pl.BlockSpec(memory_space=pltpu.VMEM)
    hbm = pl.BlockSpec(memory_space=pltpu.HBM)
    sem = pltpu.SemaphoreType.DMA
    V = pltpu.VMEM
    shape = jax.ShapeDtypeStruct
    return pl.pallas_call(
        layer_kernel,
        out_shape=(
            shape((128, 1024), BF),
            shape((128, 768), BF),
            shape((2, 12, 4, 16, 1024), BF),
            shape((1, 1024), F32),
        ),
        in_specs=[vmem, vmem, vmem, hbm, hbm, vmem, vmem],
        out_specs=(vmem, vmem, vmem, vmem),
        scratch_shapes=[
            V((768, 1024), BF), V((768, 1024), BF), sem((3,)),
            V((3, 2048, 256), BF), V((3, 128, 256), BF), V((3, 4, 256, 256), BF),
            V((3, 3, 256, 256), BF), V((3, 128, 256), BF), V((3, 128, 256), BF),
            V((3, 2, 8, 128), F32), V((8, 128), F32), V((2, 8, 128), F32), V((128, 768), F32),
            V((3, 2, 128, 256), F32),
            V((128, 1024), BF), V((128, 1024), BF), V((768, 1024), BF), V((4, 3, 64, 128), BF), V((4, 3, 64, 128), BF),
            V((128, 768), BF), V((128, 1024), BF), V((128, 768), BF), V((128, 1024), BF),
            V((768, 1024), BF), V((768, 1024), BF), V((768, 1024), BF),
            V((9, 64, 1024), BF), V((3, 64, 1024), F32), V((9, 16, 1024), F32), V((3, 16, 1024), F32),
            V((9, 16, 256), F32), V((12, 4, 16, 1024), BF), V((12, 4, 16, 1024), BF),
            V((3, 4, 2, 2, 256, 128), BF), V((3, 4, 2, 256, 128), BF), V((3, 4, 2, 256, 128), BF),
            V((3, 3, 2, 256, 128), BF), V((3, 2, 256, 128), F32), V((3, 256, 128), BF), V((3, 256, 128), BF),
            V((1, 1024), F32), V((4, 8, 128), F32), V((4, 8, 128), F32), V((4, 8, 128), F32), V((2, 8, 128), F32),
        ]
        + [sem((3,))] * 2 + [sem((24,))] * 4 + [sem((12,))] * 2 + [sem((4,))] * 2 + [sem((12,))] * 2
        + [sem((3,))] * 4 + [sem((24,))] * 2 + [sem((4,))] * 2 + [sem((3,))] * 2
        + [sem((9,))] * 12 + [sem((12,))] * 2 + [sem((10,))] * 2 + [sem((12,))] * 4 + [sem((3,))] * 2
        ,
        compiler_params=pltpu.CompilerParams(
            collective_id=0, has_side_effects=True, vmem_limit_bytes=LAYER_VMEM * 1024 * 1024
        ),
        name="layer",
    )(tile, mass, features, w_neigh, w_self, bias, cotangent)


def local(
    features, w_neigh, w_self, bias, cotangent, block_rows, block_cols, block_vals, block_count
):
    row_size = lax.axis_size("row")
    col_size = lax.axis_size("col")
    node_dev = features.shape[0]
    tile, mass = densify(
        block_vals[0, 0], block_rows[0, 0], block_cols[0, 0], block_count[0], col_size, row_size
    )
    output, grad_input, grads, g_bias = layer(
        tile, mass, features, w_neigh, w_self, bias.reshape(1, -1), cotangent
    )
    factor = 1.0 / math.sqrt(node_dev * row_size * col_size)
    grad_self, grad_neigh, output, grad_input, g_bias = finish(
        grads.reshape(2, 768, 1024), output, grad_input, g_bias, factor, 32.0 * factor
    )
    return output, grad_input, grad_self, grad_neigh, g_bias.reshape(-1)


def solution(mesh):
    in_specs = (
        P(("col", "row"), None),
        P(),
        P(),
        P(),
        P(("row", "col"), None),
        P("row", "col", None),
        P("row", "col", None),
        P("row", "col", None, None, None),
        P("row", "col"),
    )
    out_specs = (P(("row", "col"), None), P(("col", "row"), None), P(), P(), P())
    return jax.shard_map(local, mesh=mesh, in_specs=in_specs, out_specs=out_specs, check_vma=False)
```

```python
import functools
import math

import jax
import jax.numpy as jnp
from jax import lax
from jax.experimental import pallas as pl
from jax.experimental.pallas import tpu as pltpu
from jax.sharding import PartitionSpec as P


def densify_kernel(
    rows_hbm, cols_hbm, count_hbm, vals_hbm, tile, mass_ref,
    rows_ref, cols_ref, count_ref, vals, acc, in_sem, id_sem,
):
    row_blocks, col_blocks, size, _ = acc.shape
    pieces = 4
    span = vals.shape[0] // pieces

    def load(q):
        slots = pl.ds(q * span, span)
        return pltpu.make_async_copy(vals_hbm.at[slots], vals.at[slots], in_sem.at[q])

    ids = [
        pltpu.make_async_copy(rows_hbm, rows_ref, id_sem.at[0]),
        pltpu.make_async_copy(cols_hbm, cols_ref, id_sem.at[1]),
        pltpu.make_async_copy(count_hbm, count_ref, id_sem.at[2]),
    ]
    for copy in ids:
        copy.start()
    for q in range(pieces):
        load(q).start()

    def clear(i, carry):
        for j in range(col_blocks):
            acc[i, j] = jnp.zeros((size, size), jnp.float32)
        return carry

    lax.fori_loop(0, row_blocks, clear, 0)

    def add(s, carry):
        i = rows_ref[s]
        j = cols_ref[s]
        acc[i, j] += vals[s].astype(jnp.float32)
        return carry

    for copy in ids:
        copy.wait()
    count = count_ref[0]
    for q in range(pieces):
        load(q).wait()
        lax.fori_loop(q * span, jnp.minimum(count, (q + 1) * span), add, 0)
    diagonal = lax.broadcasted_iota(jnp.int32, (size, size), 0) == lax.broadcasted_iota(
        jnp.int32, (size, size), 1
    )

    def finish(i, carry):
        total = jnp.zeros((size, size), jnp.float32)
        start = pl.multiple_of(i * size, size)
        for j in range(col_blocks):
            block = acc[i, j]
            total = total + block
            tile[pl.ds(start, size), j * size : (j + 1) * size] = block.astype(jnp.bfloat16)
        sums = jnp.sum(total, axis=1, keepdims=True)
        as_row = jnp.sum(jnp.where(diagonal, sums, 0.0), axis=0, keepdims=True)
        mass_ref[i] = jnp.broadcast_to(as_row, (8, size))
        return carry

    lax.fori_loop(0, row_blocks, finish, 0)


def densify(values, row_ids, col_ids, live_count, row_blocks, col_blocks):
    slots, size, _ = values.shape
    hbm = pl.BlockSpec(memory_space=pltpu.HBM)
    vmem = pl.BlockSpec(memory_space=pltpu.VMEM)
    rows, cols = row_blocks * size, col_blocks * size
    return pl.pallas_call(
        densify_kernel,
        out_shape=(
            jax.ShapeDtypeStruct((rows, cols), jnp.bfloat16),
            jax.ShapeDtypeStruct((row_blocks, 8, size), jnp.float32),
        ),
        in_specs=[hbm, hbm, hbm, hbm],
        out_specs=(vmem, vmem),
        scratch_shapes=[
            pltpu.SMEM((slots,), jnp.int32),
            pltpu.SMEM((slots,), jnp.int32),
            pltpu.SMEM((1,), jnp.int32),
            pltpu.VMEM((slots, size, size), jnp.bfloat16),
            pltpu.VMEM((row_blocks, col_blocks, size, size), jnp.float32),
            pltpu.SemaphoreType.DMA((4,)),
            pltpu.SemaphoreType.DMA((3,)),
        ],
        compiler_params=pltpu.CompilerParams(vmem_limit_bytes=18 * 1024 * 1024),
        name="densify",
    )(row_ids, col_ids, live_count, values)


def finish_kernel(
    own_scale, neigh_scale, grads, out_in, gin_in, bias_in,
    own_to, neigh_to, out_to, gin_to, bias_to, wide, out_sem,
):
    pieces = out_sem.shape[0]
    rows = grads.shape[1]
    step = 2 * rows // pieces
    stores = []
    for p in range(pieces):
        which, at = p % 2, pl.ds(p // 2 * step, step)
        target = (own_to, neigh_to)[which]
        scale = (own_scale, neigh_scale)[which]
        wide[which, at] = grads[which, at].astype(jnp.float32) * scale
        stores.append(pltpu.make_async_copy(wide.at[which, at], target.at[at], out_sem.at[p]))
        stores[p].start()
    bias_to[...] = bias_in[...] * own_scale
    out_to[...] = out_in[...]
    gin_to[...] = gin_in[...]
    for copy in stores:
        copy.wait()


def finish(grads, output, grad_input, g_bias, own_scale, neigh_scale):
    _, rows, cols = grads.shape
    hbm = pl.BlockSpec(memory_space=pltpu.HBM)
    vmem = pl.BlockSpec(memory_space=pltpu.VMEM)
    shape = jax.ShapeDtypeStruct
    wide = shape((rows, cols), jnp.float32)
    pieces = 12
    return pl.pallas_call(
        functools.partial(finish_kernel, own_scale, neigh_scale),
        out_shape=(
            wide,
            wide,
            shape(output.shape, output.dtype),
            shape(grad_input.shape, grad_input.dtype),
            shape(g_bias.shape, g_bias.dtype),
        ),
        in_specs=[vmem, vmem, vmem, vmem],
        out_specs=(hbm, hbm, vmem, vmem, vmem),
        scratch_shapes=[
            pltpu.VMEM((2, rows, cols), jnp.float32),
            pltpu.SemaphoreType.DMA((pieces,)),
        ],
        compiler_params=pltpu.CompilerParams(vmem_limit_bytes=24 * 1024 * 1024),
        name="finish",
    )(grads, output, grad_input, g_bias)


MESH = pl.DeviceIdType.MESH
LAYER_VMEM = 36
BF = jnp.bfloat16
F32 = jnp.float32


def remote(src, dst, send, recv, device):
    return pltpu.make_async_remote_copy(
        src_ref=src, dst_ref=dst, send_sem=send, recv_sem=recv, device_id=device, device_id_type=MESH
    )


def layer_kernel(
    tile, mass, features, wn_hbm, ws_hbm, bias, cotangent,
    out_ref, gin_ref, g_ref, gbias_ref,
    wn, ws, local_sem,
    fg, own_feat, send_blocks, recv_blocks, cross_send, cross_recv,
    mass_recv, mass_cross, mass_sum, mixed, group,
    scaled, grounded, sgt, tblock, trecv,
    x_mine, y_mine, x_other, y_other, other, other_recv, partial,
    r1, q1, r2, q2, r3, result, result2,
    halves, pair_recv, row_send, row_recv, row_group, side_send, side_recv,
    bsum, bx, by, bz, bk,
    gx_s, gx_r, gz_s, gz_r, fw_s, fw_r, pm_s, pm_r, ms_s, ms_r, rs_s, rs_r, rx_s, rx_r,
    sx_s, sx_r, sy_s, sy_r, t_s, t_r,
    ot_s, ot_r, a1_s, a1_r, a2_s, a2_r, a3_s, a3_r, g3_s, g3_r, g2_s, g2_r, g1_s, g1_r, fin_s, fin_r,
    b_s, b_r, pd_s, pd_r, rz_s, rz_r, rl_s, rl_r,
):
    r = lax.axis_index("row")
    c = lax.axis_index("col")
    xl, z, core = r // 8, (r // 2) % 4, r % 2
    y, xh = c // 2, c % 2
    x = xh * 2 + xl

    def device_of(px, py, pz):
        return (((px % 2) * 4 + pz) * 2 + core, py * 2 + px // 2)

    here = (x, y, z)
    axis_orders = ((0, 1, 2), (2, 0, 1), (0, 1, 2))
    gather_orders = ((2, 1, 0), (1, 0, 2), (2, 0, 1))

    def along(axis, d):
        spot = list(here)
        spot[axis] = (spot[axis] + d) % 4
        return device_of(*spot)

    partner = (r + 1 - 2 * core, c)
    here_id = r * 8 + c
    block = r * 8 + c
    first, first_col = block % 16, block // 16

    def target(d):
        from_row = (xl * 4 + (z + 4 - d) % 4) * 2 + core
        node = c * 16 + from_row
        return node // 8, node % 8

    def holder(d):
        chip = first // 8 * 4 + (first // 2 + d) % 4
        return chip * 2 + first % 2, first_col

    def is_here(device):
        return device[0] * 8 + device[1] == here_id

    copies = [
        pltpu.make_async_copy(ws_hbm, ws, local_sem.at[1]),
        pltpu.make_async_copy(wn_hbm, wn, local_sem.at[2]),
    ]
    for copy in copies:
        copy.start()

    barrier = pltpu.get_barrier_semaphore()

    def hello(device):
        pl.semaphore_signal(barrier, inc=1, device_id=device, device_id_type=MESH)

    x_side = (((1 - xl) * 4 + z) * 2 + core, c)
    far_side = (r, y * 2 + 1 - xh)

    def z_peer(d):
        return ((xl * 4 + (z + d) % 4) * 2 + core, c)

    def y_peer(d):
        return (r, ((y + d) % 4) * 2 + xh)

    for d in range(1, 4):
        hello(z_peer(d))
        hello(y_peer(d))
    hello(x_side)
    hello(far_side)
    hello(partner)
    hello((((1 - xl) * 4 + z) * 2 + core, y * 2 + 1 - xh))

    remote_peers = 10
    for d in range(4):
        for device in (target(d), holder(d)):
            away = jnp.logical_not(is_here(device))
            remote_peers = remote_peers + away.astype(jnp.int32)

            @pl.when(away)
            def _():
                hello(device)

    pl.semaphore_wait(barrier, remote_peers)

    for n in range(3):
        fg[n, pl.ds(r * 128, 128), :] = features[:, n * 256 : (n + 1) * 256]

    def source_rows_start(s, d, k):
        chip = ((xl + s) % 2) * 4 + (z + 4 - d) % 4
        return (chip * 2 + k) * 128

    def source_rows(s, d, k):
        return pl.ds(pl.multiple_of(source_rows_start(s, d, k), 128), 128)

    def side_gather(n):
        ref = fg.at[n, source_rows(0, 0, core)]
        return remote(ref, ref, gx_s.at[n], gx_r.at[n], x_side)

    def gather_send(n, s, d):
        m = (n * 2 + s) * 4 + d
        ref = fg.at[n, source_rows(s, 0, core)]
        return remote(ref, ref, gz_s.at[m], gz_r.at[m], z_peer(d))

    def gather_recv(n, s, d):
        m = (n * 2 + s) * 4 + d
        ref = fg.at[n, source_rows(s, d, core)]
        return remote(ref, ref, gz_s.at[m], gz_r.at[m], z_peer(d))

    def forward(n, s, d):
        m = (n * 2 + s) * 4 + d
        ref = fg.at[n, source_rows(s, d, core)]
        return remote(ref, ref, fw_s.at[m], fw_r.at[m], partner)

    def own_piece(n, d):
        return own_feat.at[n, pl.ds(d * 32, 32)]

    def permute(n, d):
        start = source_rows_start(0, d, core) + d * 32
        rows = pl.ds(pl.multiple_of(start, 32), 32)
        m = d * 3 + n
        return remote(fg.at[n, rows], own_piece(n, d), pm_s.at[m], pm_r.at[m], target(d))

    def permute_start(n):
        for d in range(4):

            @pl.when(jnp.logical_not(is_here(target(d))))
            def _():
                permute(n, d).start()

            @pl.when(is_here(target(d)))
            def _():
                start = source_rows_start(0, d, core) + d * 32
                own_feat[n, d * 32 : (d + 1) * 32, :] = fg[n, pl.ds(pl.multiple_of(start, 32), 32), :]

    def permute_wait(n):
        for d in range(4):

            @pl.when(jnp.logical_not(is_here(holder(d))))
            def _():
                permute(n, d).wait_recv()

    def mass_send(d):
        to = ((y + d) % 4) * 2
        return remote(mass.at[pl.ds(to, 2)], mass_recv.at[d - 1], ms_s.at[d], ms_r.at[d], y_peer(d))

    def mass_side():
        return remote(mass_sum.at[1 - xh], mass_cross, ms_s.at[0], ms_r.at[0], far_side)

    def spread_gather(n):
        side_gather(n).wait_recv()
        for s in range(2):
            for d in range(1, 4):
                gather_send(n, s, d).start()

    for n in range(3):
        side_gather(n).start()
    for d in range(1, 4):
        gather_send(0, 0, d).start()
    for d in range(1, 4):
        mass_send(d).start()
    side_gather(0).wait_recv()
    for d in range(1, 4):
        gather_send(0, 1, d).start()
    spread_gather(1)


    def reduce_send(n, d):
        m = n * 4 + d
        return remote(
            send_blocks.at[n, d], recv_blocks.at[n, d - 1], rs_s.at[m], rs_r.at[m], y_peer(d)
        )

    def cross(n):
        return remote(cross_send.at[n], cross_recv.at[n], rx_s.at[n], rx_r.at[n], far_side)

    def mix(n):
        for s in range(2):
            forward(n, s, 0).start()
        for s in range(2):
            for d in range(1, 4):
                gather_recv(n, s, d).wait_recv()
                forward(n, s, d).start()
        if n == 0:
            spread_gather(2)
        for s in range(2):
            for d in range(4):
                forward(n, s, d).wait_recv()

        def mix_step(t, carry):
            d = (t + 1) % 4
            rows = pl.ds(pl.multiple_of(((y + d) % 4) * 256, 256), 256)
            value = jnp.dot(tile[rows, :], fg[n], preferred_element_type=F32)

            @pl.when(t < 3)
            def _():
                send_blocks[n, d] = value.astype(BF)
                reduce_send(n, d).start()

            @pl.when(t == 3)
            def _():
                group[n, 0] = value[:128]
                group[n, 1] = value[128:]

            return carry

        lax.fori_loop(0, 4, mix_step, 0)

    def cross_start(n):
        for d in range(1, 4):
            reduce_send(n, d).wait_recv()
        for h in range(2):
            total = group[n, h]
            for d in range(3):
                total = total + recv_blocks[n, d, h * 128 : (h + 1) * 128].astype(F32)
            group[n, h] = total
        cross_send[n] = group[n, 1 - xh].astype(BF)
        cross(n).start()

    mix(0)
    mix(1)
    cross_start(0)
    for d in range(1, 4):
        mass_send(d).wait_recv()
    for h in range(2):
        mass_sum[h] = mass[y * 2 + h] + ((mass_recv[0, h] + mass_recv[1, h]) + mass_recv[2, h])
    mass_side().start()
    mix(2)
    permute_start(0)
    permute_start(1)
    permute_start(2)
    cross_start(1)
    cross_start(2)
    for copy in copies:
        copy.wait()

    for n in range(3):
        permute_wait(n)
    mass_side().wait_recv()
    degree = mass_sum[xh] + mass_cross[...]
    for n in range(3):
        cross(n).wait_recv()
        mixed[:, n * 256 : (n + 1) * 256] = group[n, xh] + cross_recv[n].astype(F32)

    diagonal = lax.broadcasted_iota(jnp.int32, (128, 128), 0) == lax.broadcasted_iota(
        jnp.int32, (128, 128), 1
    )
    column = jnp.sum(jnp.where(diagonal, degree[0:1, :], 0.0), axis=1, keepdims=True)
    inverse = 1.0 / (column + 1.0)
    high = mixed[...].astype(BF)
    low = (mixed[...] - high.astype(F32)).astype(BF)
    mixed_high = x_other
    mixed_high[...] = high
    x_mine[...] = low

    def layer_step(n, carry):
        cols = pl.ds(pl.multiple_of(n * 256, 256), 256)
        aggregate = jnp.dot(mixed_high[...], wn[:, cols], preferred_element_type=F32)
        aggregate += jnp.dot(x_mine[...], wn[:, cols], preferred_element_type=F32)
        own = jnp.dot(own_feat[0], ws[0:256, cols], preferred_element_type=F32)
        own += jnp.dot(own_feat[1], ws[256:512, cols], preferred_element_type=F32)
        own += jnp.dot(own_feat[2], ws[512:768, cols], preferred_element_type=F32)
        preact = own.astype(BF).astype(F32) + aggregate * inverse + bias[:, cols]
        small = jnp.exp(jnp.minimum(preact, 0.0))
        above = preact > 0
        out_ref[:, cols] = jnp.where(above, preact, small - 1.0).astype(BF)
        grad = cotangent[:, cols].astype(F32) * jnp.where(above, 1.0, small)
        grounded[:, cols] = grad.astype(BF)
        scaled[:, cols] = (grad * inverse).astype(BF)
        bsum[:, cols] = jnp.sum(grad, axis=0, keepdims=True)
        return carry

    lax.fori_loop(0, 4, layer_step, 0)

    lanes = pl.ds(pl.multiple_of(c * 128, 128), 128)
    turned = (((1,), (1,)), ((), ()))

    def spread_ref(n, s, d):
        who = ((y + 4 - d) % 4) * 2 + (xh + s) % 2
        return sgt.at[pl.ds(n * 256, 256), pl.ds(pl.multiple_of(who * 128, 128), 128)]

    def spread_side(n):
        ref = spread_ref(n, 0, 0)
        return remote(ref, ref, sx_s.at[n], sx_r.at[n], far_side)

    def spread_send(n, s, d):
        m = (n * 2 + s) * 4 + d
        ref = spread_ref(n, s, 0)
        return remote(ref, ref, sy_s.at[m], sy_r.at[m], y_peer(d))

    def spread_recv(n, s, d):
        m = (n * 2 + s) * 4 + d
        ref = spread_ref(n, s, d)
        return remote(ref, ref, sy_s.at[m], sy_r.at[m], y_peer(d))

    def spread_more(n, sides):
        for s in sides:
            if s == 1:
                spread_side(n).wait_recv()
            for d in range(1, 4):
                spread_send(n, s, d).start()

    for n in range(3):
        part_rows = pl.ds(n * 256, 256)
        sgt[part_rows, lanes] = lax.dot_general(
            wn[part_rows, :], scaled[...], turned, preferred_element_type=F32
        ).astype(BF)
        spread_side(n).start()
        if n == 0:
            spread_more(0, (0,))
    def self_send(d):
        return remote(tblock.at[d], trecv.at[d], t_s.at[d], t_r.at[d], holder(d))

    def self_wait():
        for d in range(4):

            @pl.when(jnp.logical_not(is_here(target(d))))
            def _():
                self_send(d).wait_recv()

    flipped = (((0,), (0,)), ((), ()))

    def part(j):
        return pl.ds(j * 256, 256)

    def other_send(j):
        return remote(other.at[part(j)], other_recv.at[part(j)], ot_s.at[j], ot_r.at[j], partner)

    def ar_other():
        @pl.when(core == 0)
        def _():
            for n in range(3):
                x_mine[:, n * 256 : (n + 1) * 256] = own_feat[n]
            y_mine[...] = grounded[...]
            y_other[...] = scaled[...]

        @pl.when(core == 1)
        def _():
            x_mine[...] = x_other[...]
            for n in range(3):
                x_other[:, n * 256 : (n + 1) * 256] = own_feat[n]
            y_mine[...] = scaled[...]
            y_other[...] = grounded[...]

        for j in range(3):
            other[part(j), :] = lax.dot_general(
                x_other[:, part(j)], y_other[...], flipped, preferred_element_type=F32
            ).astype(BF)
            other_send(j).start()

    def stage1(j, d):
        axis = axis_orders[j][0]
        rows = pl.ds(pl.multiple_of(j * 256 + ((here[axis] + d) % 4) * 64, 64), 64)
        n = j * 3 + d - 1
        return remote(partial.at[rows], r1.at[n], a1_s.at[n], a1_r.at[n], along(axis, d))

    bias_slots = (bx, by, bz)

    def bias_send(axis, d):
        n = axis * 3 + d - 1
        slot = bias_slots[axis].at[here[axis]]
        return remote(slot, slot, b_s.at[n], b_r.at[n], along(axis, d))

    def bias_recv(axis, d):
        n = axis * 3 + d - 1
        slot = bias_slots[axis].at[(here[axis] + 4 - d) % 4]
        return remote(slot, slot, b_s.at[n], b_r.at[n], along(axis, d))

    def bias_start(axis, value):
        bias_slots[axis][here[axis]] = value
        for d in range(1, 4):
            bias_send(axis, d).start()

    def bias_total(axis):
        for d in range(1, 4):
            bias_recv(axis, d).wait_recv()
        slots = bias_slots[axis]
        return (slots[0] + slots[1]) + (slots[2] + slots[3])

    def ar_mine():
        for j in range(3):
            mine_part = lax.dot_general(
                x_mine[:, part(j)], y_mine[...], flipped, preferred_element_type=F32
            )
            other_send(j).wait_recv()
            partial[part(j), :] = (mine_part + other_recv[part(j), :].astype(F32)).astype(BF)
            for d in range(1, 4):
                stage1(j, d).start()

        bias_start(0, jnp.concatenate([bsum[:, i * 128 : (i + 1) * 128] for i in range(8)], axis=0))

    def pair_send(n, d):
        m = n * 4 + d
        return remote(halves.at[n, d, 1 - core], pair_recv.at[n, d], pd_s.at[m], pd_r.at[m], partner)

    def row_out(n, d):
        m = n * 4 + d
        return remote(row_send.at[n, d], row_recv.at[n, d - 1], rz_s.at[m], rz_r.at[m], z_peer(d))

    def row_side(n):
        return remote(side_send.at[n], side_recv.at[n], rl_s.at[n], rl_r.at[n], x_side)

    def pair_sum(n, d):
        pair_send(n, d).wait_recv()
        row_group[n] = halves[n, d, core].astype(F32) + pair_recv[n, d].astype(F32)
        q = (4 - d) % 4
        rows = pl.ds(pl.multiple_of(q * 64, 64), 64)
        row_group[n, xl, rows, :] = row_group[n, xl, rows, :] + trecv[q, n].astype(F32)
        return row_group[n]

    def back(n):
        for s in range(2):
            for d in range(1, 4):
                spread_recv(n, s, d).wait_recv()

        def back_step(t, carry):
            d = (t + 1) % 4
            for side in range(2):
                chip = side * 4 + (z + d) % 4
                where = pl.ds(pl.multiple_of(chip * 256, 256), 256)
                value = jnp.dot(
                    sgt[n * 256 : (n + 1) * 256, :], tile[:, where], preferred_element_type=F32
                )
                halves[n, d, 0, side] = value[:, :128].astype(BF)
                halves[n, d, 1, side] = value[:, 128:].astype(BF)
            pair_send(n, d).start()
            return carry

        lax.fori_loop(0, 4, back_step, 0)

        def pair_step(d, carry):
            row_send[n, d] = pair_sum(n, d).astype(BF)
            row_out(n, d).start()
            return carry

        lax.fori_loop(1, 4, pair_step, 0)
        pair_sum(n, 0)

    def row_cross(n):
        for d in range(1, 4):
            row_out(n, d).wait_recv()
        total = row_group[n]
        for d in range(3):
            total = total + row_recv[n, d].astype(F32)
        row_group[n] = total
        side_send[n] = row_group[n, 1 - xl].astype(BF)
        row_side(n).start()

    def row_finish(n):
        rows = slice(n * 256, (n + 1) * 256)
        row_side(n).wait_recv()
        total = row_group[n, xl] + side_recv[n].astype(F32)
        gin_ref[:, rows] = total.T.astype(BF)

    def stage2(j, d):
        axis = axis_orders[j][1]
        rows = pl.ds(pl.multiple_of(((here[axis] + d) % 4) * 16, 16), 16)
        n = j * 3 + d - 1
        return remote(q1.at[j, rows], r2.at[n], a2_s.at[n], a2_r.at[n], along(axis, d))

    def stage3(j, d):
        axis = axis_orders[j][2]
        cols = pl.ds(pl.multiple_of(((here[axis] + d) % 4) * 256, 256), 256)
        n = j * 3 + d - 1
        return remote(q2.at[j, :, cols], r3.at[n], a3_s.at[n], a3_r.at[n], along(axis, d))

    def ar_sum1():
        for j in range(3):
            axis = axis_orders[j][0]
            for d in range(1, 4):
                stage1(j, d).wait_recv()
            rows = pl.ds(pl.multiple_of(j * 256 + here[axis] * 64, 64), 64)
            total = partial[rows, :].astype(F32)
            for d in range(3):
                total = total + r1[j * 3 + d].astype(F32)
            q1[j] = total
            for d in range(1, 4):
                stage2(j, d).start()
        bias_start(1, bias_total(0))

    def ar_sum2():
        for j in range(3):
            axis = axis_orders[j][1]
            for d in range(1, 4):
                stage2(j, d).wait_recv()
            total = q1[j, pl.ds(pl.multiple_of(here[axis] * 16, 16), 16), :]
            for d in range(3):
                total = total + r2[j * 3 + d]
            q2[j] = total
            for d in range(1, 4):
                stage3(j, d).start()
        bias_start(2, bias_total(1))

    def place(j, shift, step):
        a, b, e = axis_orders[j]
        order = gather_orders[j]
        spot = list(here)
        spot[order[step]] = (spot[order[step]] + 4 - shift) % 4
        lead = j * 4 + spot[a]
        if step == 0:
            return result.at[lead, spot[b], :, pl.ds(pl.multiple_of(spot[e] * 256, 256), 256)]
        if step == 1:
            return result.at[lead, spot[b]]
        return final(result, j, spot)

    def final(ref, j, spot):
        a, b, e = axis_orders[j]
        if gather_orders[j][2] == a:
            return ref.at[j * 4 + spot[a]]
        return ref.at[pl.ds(j * 4, 4), spot[b]]

    def back_copy(j, d, step, shift, sends, recvs):
        n = j * 3 + d - 1
        ref = place(j, shift, step)
        return remote(ref, ref, sends.at[n], recvs.at[n], along(gather_orders[j][step], d))

    def bias_pair(slot):
        return remote(bk.at[slot], bk.at[slot], b_s.at[9], b_r.at[9], partner)

    def ar_sum3():
        for j in range(3):
            axis = axis_orders[j][2]
            for d in range(1, 4):
                stage3(j, d).wait_recv()
            cols = pl.ds(pl.multiple_of(here[axis] * 256, 256), 256)
            total = q2[j, :, cols]
            for d in range(3):
                total = total + r3[j * 3 + d]
            place(j, 0, 0)[...] = total.astype(BF)
            for d in range(1, 4):
                back_copy(j, d, 0, 0, g3_s, g3_r).start()
        bias_core = bias_total(2)
        bk[core] = bias_core

        bias_pair(core).start()

    def ar_gather2():
        for j in range(3):
            for d in range(1, 4):
                back_copy(j, d, 0, d, g3_s, g3_r).wait_recv()
            for d in range(1, 4):
                back_copy(j, d, 1, 0, g2_s, g2_r).start()

    def ar_gather1():
        for j in range(3):
            for d in range(1, 4):
                back_copy(j, d, 1, d, g2_s, g2_r).wait_recv()
            for d in range(1, 4):
                back_copy(j, d, 2, 0, g1_s, g1_r).start()

    def last_spot(j, d):
        axis = gather_orders[j][2]
        spot = list(here)
        spot[axis] = (spot[axis] + 4 - d) % 4
        return spot

    def finish_copy(j, d):
        n = j * 4 + d
        spot = last_spot(j, d)
        return remote(
            final(result, j, spot), final(result2, j, spot), fin_s.at[n], fin_r.at[n], partner
        )

    def own_out(j, d):
        spot = last_spot(j, d)
        final(g_ref.at[core], j, spot)[...] = final(result, j, spot)[...]

    def pair_out(j, d):
        spot = last_spot(j, d)
        final(g_ref.at[1 - core], j, spot)[...] = final(result2, j, spot)[...]

    def ar_hand():
        for j in range(3):
            finish_copy(j, 0).start()
            own_out(j, 0)

    def ar_finish():
        for j in range(3):
            for d in range(1, 4):
                back_copy(j, d, 2, d, g1_s, g1_r).wait_recv()
                finish_copy(j, d).start()
                own_out(j, d)
        bias_pair(1 - core).wait_recv()
        total = bk[0] + bk[1]
        gbias_ref[...] = jnp.concatenate([total[i : i + 1, :] for i in range(8)], axis=1)
        for j in range(3):
            for d in range(4):
                finish_copy(j, d).wait_recv()
                pair_out(j, d)

    def self_start():
        for n in range(3):
            part_rows = pl.ds(n * 256, 256)
            value = lax.dot_general(
                ws[part_rows, :], grounded[...], turned, preferred_element_type=F32
            ).astype(BF)
            for d in range(4):
                tblock[d, n] = value[d * 64 : (d + 1) * 64]

        for d in range(4):

            @pl.when(jnp.logical_not(is_here(holder(d))))
            def _():
                self_send(d).start()

            @pl.when(is_here(holder(d)))
            def _():
                trecv[d] = tblock[d]

    def drain_own():
        for d in range(4):

            @pl.when(jnp.logical_not(is_here(target(d))))
            def _():
                for n in range(3):
                    permute(n, d).wait_send()

            @pl.when(jnp.logical_not(is_here(holder(d))))
            def _():
                self_send(d).wait_send()

    def drain_forward():
        for n in range(3):
            side_gather(n).wait_send()
            cross(n).wait_send()
            for d in range(1, 4):
                reduce_send(n, d).wait_send()
            for s in range(2):
                for d in range(1, 4):
                    gather_send(n, s, d).wait_send()
                for d in range(4):
                    forward(n, s, d).wait_send()
        for d in range(1, 4):
            mass_send(d).wait_send()
        mass_side().wait_send()

    def drain_back():
        for n in range(3):
            spread_side(n).wait_send()
            row_side(n).wait_send()
            for d in range(4):
                pair_send(n, d).wait_send()
            for d in range(1, 4):
                row_out(n, d).wait_send()
                for s in range(2):
                    spread_send(n, s, d).wait_send()

    def drain_ar():
        for j in range(3):
            other_send(j).wait_send()
            for d in range(1, 4):
                stage1(j, d).wait_send()
                stage2(j, d).wait_send()
                stage3(j, d).wait_send()
                back_copy(j, d, 0, 0, g3_s, g3_r).wait_send()
                back_copy(j, d, 1, 0, g2_s, g2_r).wait_send()
                bias_send(j, d).wait_send()

    def drain_last():
        for j in range(3):
            for d in range(1, 4):
                back_copy(j, d, 2, 0, g1_s, g1_r).wait_send()
            for d in range(4):
                finish_copy(j, d).wait_send()
        bias_pair(core).wait_send()

    self_start()
    spread_more(0, (1,))
    spread_more(1, (0, 1))
    ar_other()
    spread_more(2, (0, 1))
    ar_mine()
    drain_forward()
    self_wait()
    back(0)
    back(1)
    ar_sum1()
    back(2)
    row_cross(0)
    ar_sum2()
    row_cross(1)
    ar_sum3()
    row_cross(2)
    ar_gather2()
    ar_gather1()
    ar_hand()
    row_finish(0)
    row_finish(1)
    row_finish(2)
    drain_own()
    drain_back()
    drain_ar()
    ar_finish()
    drain_last()


def layer(tile, mass, features, w_neigh, w_self, bias, cotangent):
    vmem = pl.BlockSpec(memory_space=pltpu.VMEM)
    hbm = pl.BlockSpec(memory_space=pltpu.HBM)
    sem = pltpu.SemaphoreType.DMA
    V = pltpu.VMEM
    shape = jax.ShapeDtypeStruct
    return pl.pallas_call(
        layer_kernel,
        out_shape=(
            shape((128, 1024), BF),
            shape((128, 768), BF),
            shape((2, 12, 4, 16, 1024), BF),
            shape((1, 1024), F32),
        ),
        in_specs=[vmem, vmem, vmem, hbm, hbm, vmem, vmem],
        out_specs=(vmem, vmem, vmem, vmem),
        scratch_shapes=[
            V((768, 1024), BF), V((768, 1024), BF), sem((3,)),
            V((3, 2048, 256), BF), V((3, 128, 256), BF), V((3, 4, 256, 256), BF),
            V((3, 3, 256, 256), BF), V((3, 128, 256), BF), V((3, 128, 256), BF),
            V((3, 2, 8, 128), F32), V((8, 128), F32), V((2, 8, 128), F32), V((128, 768), F32),
            V((3, 2, 128, 256), F32),
            V((128, 1024), BF), V((128, 1024), BF), V((768, 1024), BF), V((4, 3, 64, 128), BF), V((4, 3, 64, 128), BF),
            V((128, 768), BF), V((128, 1024), BF), V((128, 768), BF), V((128, 1024), BF),
            V((768, 1024), BF), V((768, 1024), BF), V((768, 1024), BF),
            V((9, 64, 1024), BF), V((3, 64, 1024), F32), V((9, 16, 1024), F32), V((3, 16, 1024), F32),
            V((9, 16, 256), F32), V((12, 4, 16, 1024), BF), V((12, 4, 16, 1024), BF),
            V((3, 4, 2, 2, 256, 128), BF), V((3, 4, 2, 256, 128), BF), V((3, 4, 2, 256, 128), BF),
            V((3, 3, 2, 256, 128), BF), V((3, 2, 256, 128), F32), V((3, 256, 128), BF), V((3, 256, 128), BF),
            V((1, 1024), F32), V((4, 8, 128), F32), V((4, 8, 128), F32), V((4, 8, 128), F32), V((2, 8, 128), F32),
        ]
        + [sem((3,))] * 2 + [sem((24,))] * 4 + [sem((12,))] * 2 + [sem((4,))] * 2 + [sem((12,))] * 2
        + [sem((3,))] * 4 + [sem((24,))] * 2 + [sem((4,))] * 2 + [sem((3,))] * 2
        + [sem((9,))] * 12 + [sem((12,))] * 2 + [sem((10,))] * 2 + [sem((12,))] * 4 + [sem((3,))] * 2
        ,
        compiler_params=pltpu.CompilerParams(
            collective_id=0, has_side_effects=True, vmem_limit_bytes=LAYER_VMEM * 1024 * 1024
        ),
        name="layer",
    )(tile, mass, features, w_neigh, w_self, bias, cotangent)


def local(
    features, w_neigh, w_self, bias, cotangent, block_rows, block_cols, block_vals, block_count
):
    row_size = lax.axis_size("row")
    col_size = lax.axis_size("col")
    node_dev = features.shape[0]
    tile, mass = densify(
        block_vals[0, 0], block_rows[0, 0], block_cols[0, 0], block_count[0], col_size, row_size
    )
    output, grad_input, grads, g_bias = layer(
        tile, mass, features, w_neigh, w_self, bias.reshape(1, -1), cotangent
    )
    factor = 1.0 / math.sqrt(node_dev * row_size * col_size)
    grad_self, grad_neigh, output, grad_input, g_bias = finish(
        grads.reshape(2, 768, 1024), output, grad_input, g_bias, factor, 32.0 * factor
    )
    return output, grad_input, grad_self, grad_neigh, g_bias.reshape(-1)


def solution(mesh):
    in_specs = (
        P(("col", "row"), None),
        P(),
        P(),
        P(),
        P(("row", "col"), None),
        P("row", "col", None),
        P("row", "col", None),
        P("row", "col", None, None, None),
        P("row", "col"),
    )
    out_specs = (P(("row", "col"), None), P(("col", "row"), None), P(), P(), P())
    return jax.shard_map(local, mesh=mesh, in_specs=in_specs, out_specs=out_specs, check_vma=False)
```
